256 devices in a mesh: half: 2 (over core), seq: 8 (over z), exp: 16 (over y, x).
Axes of the slice: x: 4, y: 4, z: 8, core: 2. Of those that a mesh axis runs over, the one named last changes fastest.
Arguments:
- prompt_hidden: bfloat16 [2, 8, 16, 256, 5120], P('half', 'seq', 'exp'), may hold values from -6 to 6
- decode_hidden: bfloat16 [2, 8, 16, 4, 5120], P('half', 'seq', 'exp'), may hold values from -6 to 6
- norm_gain: float32 [5120], replicated, may hold values from 0.1 to 1.9
- w_dkv: bfloat16 [5120, 576], replicated, may hold values from -0.078125 to 0.078125
- kv_gain: float32 [512], replicated, may hold values from 0.1 to 1.9
- w_gate: bfloat16 [16, 5120, 1536], P('exp', None, 'seq'), may hold values from -0.078125 to 0.078125
- w_up: bfloat16 [16, 5120, 1536], P('exp', None, 'seq'), may hold values from -0.078125 to 0.078125
- w_down: bfloat16 [16, 1536, 5120], P('exp', 'seq'), may hold values from -0.15625 to 0.15625
- expert_ids: int32 [2, 8, 16, 4, 6], P('half', 'seq', 'exp'), may hold values from 0 to 15, all different within a row; in each aligned block of 4 rows (0 to 3, 4 to 7, ..., all dimensions but the last counted through in order) at most 2 rows name the same one
- gate_values: float32 [2, 8, 16, 4, 6], P('half', 'seq', 'exp'), may hold values from 0.05 to 0.6
- owner: int32 [16, 16], replicated, may hold values from 0 to 15, each once within a row
- prompt_lengths: int32 [256], replicated, may hold values from 64 to 256
- context_lengths: int32 [2, 8, 16, 2], P('half', 'seq', 'exp'), may hold values from 1 to 4095
Outputs:
- moe_out: bfloat16 [2, 8, 16, 4, 5120], P('half', 'seq', 'exp')
- new_latents: bfloat16 [2, 8, 16, 4, 576], P('half', 'seq', 'exp')
- owner_cache: bfloat16 [2, 8, 16, 256, 576], P('half', 'seq', 'exp')
The draws below stay inside these ranges and needn't reach their ends.
Inputs may be any that keep to these rules, and one draw needn't show every extreme that they name: `expert_ids`: in the 4 rows of one device no expert is named more than 2 times, a bound that some block reaches. Each row is a permutation: every owner takes exactly one prompt of each b.
All inputs are finite; a program needn't handle non-finite values.
Results may differ from the reference program's by a relative error of at most 0.017.
Values may be sent and summed in bfloat16 or wider, within the bound.
A program may use at most 128 MiB of HBM per device.

```python
import math
import jax
import jax.numpy as jnp
import numpy as np
from jax import lax

D = 5120
LAT = 512
FF = 1536
TOP = 6
EXPERTS = 16
SPAN = 1
LEN = 256
REQ = 2
ROWS = 256
DROWS = 4
CAP = 2
PGROUPS = 16
OWNERS = 16
PROMPTS = 256
LATW = 576
N_HALF = 2
N_SEQ = 8
N_EXP = 16


def touch_ends(result, key, low, high):
    dims = result.shape
    spot = [jax.random.randint(jax.random.fold_in(key, axis), (), 0, dims[axis]) for axis in range(len(dims))]
    result = result.at[tuple(spot)].set(low)
    longest = dims.index(max(dims))
    spot[longest] = (spot[longest] + 1) % dims[longest]
    return result.at[tuple(spot)].set(high)


def block_levels(key, extent, pieces, low, high):
    def one(axis_at, blocks):
        draws = jax.random.uniform(jax.random.fold_in(jax.random.fold_in(key, 6), axis_at), (blocks,), jnp.float32, low / len(pieces), high / len(pieces))
        return jnp.repeat(jnp.exp(draws), extent[axis_at] // blocks).reshape((-1,) + (1,) * (len(extent) - axis_at - 1))

    factor_of = one(*pieces[0])
    for cut in pieces[1:]:
        factor_of = factor_of * one(*cut)
    return factor_of


def shared_out(own_key, own, number, rows, amount, top, limit, lean):
    sequence = jax.random.permutation(own_key, amount)
    heavy_load, usual = load_shares(amount, rows * top, limit, lean, True), load_shares(amount, rows * top, limit, lean, False)
    places = jnp.arange(amount)

    def named(lengths, rotation):
        used = int((lengths > 0).sum())
        fixed = max(1, used // 4)
        shifted = fixed + (places - fixed + rotation * (used - fixed)) % max(1, amount - fixed)
        return jnp.zeros((amount,), jnp.int32).at[sequence[jnp.where(places < fixed, places, shifted)]].set(jnp.asarray(lengths, jnp.int32))

    lengths = jnp.where(number % 4 == 0, named(heavy_load, number // 4), named(usual, number - number // 4 - 1))
    mixed = jax.random.permutation(jax.random.fold_in(own, 3), amount)
    source_of, taker = mixed[0:amount // 2 * 2:2], mixed[1:amount // 2 * 2:2]
    slack = jnp.minimum(lengths[source_of] - 1, limit - lengths[taker]) // 2
    slack = jnp.where((source_of == sequence[0]) | (taker == sequence[0]) | (lengths[taker] == 0), 0, jnp.maximum(slack, 0))
    shifted = jax.random.randint(jax.random.fold_in(own, 4), (amount // 2,), 0, 1 << 20) % (slack + 1)
    lengths = lengths.at[source_of].add(-shifted).at[taker].add(shifted)
    members = jnp.searchsorted(jnp.cumsum(lengths), jnp.arange(rows * top), side="right").astype(jnp.int32)
    grid = members.reshape(top, rows).T
    grid = grid[jax.random.permutation(jax.random.fold_in(own, 1), rows)]
    rotation = jax.random.randint(jax.random.fold_in(own, 2), (rows, 1), 0, top)
    return jnp.take_along_axis(grid, (jnp.arange(top)[None, :] + rotation) % top, axis=1)


def load_shares(number_of, total, most, skew, full):
    portions = [(1 << 20) // math.isqrt(standing ** skew) + 1 for standing in range(1, number_of + 1)]
    largest = most if full else min(most, max(-(-total // number_of), total * portions[0] // sum(portions)))
    least = 1 if total - largest >= number_of - 1 else 0
    holding, rest = [largest] + [least] * (number_of - 1), total - largest - least * (number_of - 1)
    while rest > 0:
        movable = [i for i in range(1, number_of) if holding[i] < largest] or [i for i in range(1, number_of) if holding[i] < most]
        mass, budget = sum([portions[i] for i in movable]), rest
        for i in movable:
            extra = min(most - holding[i], max(1, budget * portions[i] // mass), rest)
            holding[i] = holding[i] + extra
            rest = rest - extra
    return np.array(holding)


def noise(rng, dims, deviation, bound, split=(), dtype=jnp.bfloat16):
    result = deviation * jax.random.normal(rng, dims, jnp.float32)
    if split:
        result = result * block_levels(rng, dims, split, -0.22, 0.18)
    return jnp.clip(result, -bound, bound).astype(dtype)


def setup_inputs(seed: int = 0) -> dict:
    seeds = jax.random.split(jax.random.key(seed), 14)
    prompt_hidden = noise(seeds[0], (N_HALF, N_SEQ, N_EXP, ROWS, D), 1.0, 6.0, ((0, 2), (1, 8), (2, 16)))
    decode_hidden = noise(seeds[1], (N_HALF, N_SEQ, N_EXP, DROWS, D), 1.0, 6.0, ((0, 2), (1, 8), (2, 16)))
    norm_gain = jnp.clip(1.0 + 0.18 * jax.random.normal(seeds[2], (D,), jnp.float32), 0.1, 1.9)
    w_dkv = noise(seeds[3], (D, LATW), D ** -0.5, 0.078125)
    kv_gain = jnp.clip(1.0 + 0.18 * jax.random.normal(seeds[4], (LAT,), jnp.float32), 0.1, 1.9)
    w_gate = noise(seeds[5], (EXPERTS, D, FF), D ** -0.5, 0.078125, ((0, 16), (2, 8)))
    w_up = noise(seeds[6], (EXPERTS, D, FF), D ** -0.5, 0.078125, ((0, 16), (2, 8)))
    w_down = noise(seeds[7], (EXPERTS, FF, D), FF ** -0.5, 0.15625, ((0, 16), (1, 8)))
    expert_ids_keys = jax.random.split(jax.random.fold_in(seeds[8], 1), N_HALF * N_SEQ * N_EXP * DROWS // DROWS)
    expert_ids_turns = jax.random.permutation(jax.random.fold_in(seeds[8], 3), N_HALF * N_SEQ * N_EXP * DROWS // DROWS)
    expert_ids = jax.vmap(lambda own, number: shared_out(jax.random.fold_in(seeds[8], 2), own, number, DROWS, EXPERTS, TOP, CAP, 2))(expert_ids_keys, expert_ids_turns).reshape((N_HALF, N_SEQ, N_EXP, DROWS, TOP))
    gate_values = jnp.clip(jnp.exp(math.log(0.6) - 2.4849067 * jax.random.uniform(seeds[9], (N_HALF, N_SEQ, N_EXP, DROWS, TOP), jnp.float32) ** block_levels(seeds[9], (N_HALF, N_SEQ, N_EXP, DROWS, TOP), ((0, 2), (1, 8), (2, 16)), -0.2, 0.2)), 0.05, 0.6)
    owner = jax.vmap(lambda own: jax.random.permutation(own, OWNERS))(jax.random.split(seeds[10], PGROUPS)).reshape((PGROUPS, OWNERS)).astype(jnp.int32)
    prompt_lengths = touch_ends(jax.random.randint(seeds[11], (PROMPTS,), LEN // 4, LEN + 1), jax.random.fold_in(seeds[11], 1), LEN // 4, LEN).astype(jnp.int32)
    context_lengths = touch_ends(jax.random.randint(seeds[12], (N_HALF, N_SEQ, N_EXP, REQ), 1, 4096), jax.random.fold_in(seeds[12], 1), 1, 4095).astype(jnp.int32)
    return {"prompt_hidden": prompt_hidden, "decode_hidden": decode_hidden, "norm_gain": norm_gain, "w_dkv": w_dkv, "kv_gain": kv_gain, "w_gate": w_gate, "w_up": w_up, "w_down": w_down, "expert_ids": expert_ids, "gate_values": gate_values, "owner": owner, "prompt_lengths": prompt_lengths, "context_lengths": context_lengths}


def rms_scale(values, gain):
    mean_sq = lax.optimization_barrier(jnp.mean(values * values, axis=-1, keepdims=True))
    return values * lax.rsqrt(mean_sq + 1e-06) * gain

def rotate_rope(values, positions):
    halfway = values.shape[-1] // 2
    freq = 10000.0 ** (-(jnp.arange(halfway).astype(jnp.float32) * 2.0 / values.shape[-1]))
    angle = positions.astype(jnp.float32)[..., None] * freq
    first = values[..., :halfway]
    second = values[..., halfway:]
    cosine = jnp.cos(angle)
    sine = jnp.sin(angle)
    return jnp.concatenate([first * cosine - second * sine, second * cosine + first * sine], axis=-1)

def make_latents(comp, positions, kv_gain):
    latent = rms_scale(comp[..., :LAT], kv_gain)
    rotated = rotate_rope(comp[..., LAT:], positions)
    return jnp.concatenate([latent, rotated], axis=-1).astype(jnp.bfloat16)

def expert_rows(rows, wgate, wup, wdown):
    gate = jnp.dot(rows, wgate, preferred_element_type=jnp.float32)
    upper = jnp.dot(rows, wup, preferred_element_type=jnp.float32)
    act = (jax.nn.silu(gate) * upper).astype(jnp.bfloat16)
    block = FF // N_SEQ
    parts = jnp.einsum('rsf,sfd->rsd', act.reshape(-1, N_SEQ, block).astype(jnp.float32), wdown.reshape(N_SEQ, block, D).astype(jnp.float32))
    parts = lax.optimization_barrier(parts.astype(jnp.bfloat16))
    return lax.optimization_barrier(jnp.sum(parts.astype(jnp.float32), axis=1)).astype(jnp.bfloat16)

def moe_half(tokens, ids, gates, w_gate, w_up, w_down):
    blocks = tokens.shape[0]
    flat = ids.reshape(blocks, DROWS * TOP)
    onehot = (flat[..., None] == jnp.arange(EXPERTS).astype(jnp.int32)).astype(jnp.int32)
    before = jnp.cumsum(onehot, axis=1) - onehot
    slot = lax.optimization_barrier(jnp.sum(before * onehot, axis=-1))
    place = (flat * CAP + slot).astype(jnp.int32)
    source_rows = jnp.repeat(tokens, TOP, axis=1)
    block_index = jnp.arange(blocks).astype(jnp.int32)[:, None]
    buffer = jnp.zeros((blocks, EXPERTS * CAP, D), jnp.bfloat16).at[block_index, place].set(source_rows)
    per_expert = buffer.reshape(blocks, EXPERTS, CAP, D).transpose(1, 0, 2, 3).reshape(EXPERTS, blocks * CAP, D)
    results = lax.map(lambda packed: expert_rows(*packed), (per_expert, w_gate, w_up, w_down))
    back = results.reshape(EXPERTS, blocks, CAP, D).transpose(1, 0, 2, 3).reshape(blocks, EXPERTS * CAP, D)
    picked = jnp.take_along_axis(back, place[..., None], axis=1)
    picked = picked.reshape(blocks, DROWS, TOP, D).astype(jnp.float32)
    weights = gates.reshape(blocks, DROWS, TOP, 1)
    return lax.optimization_barrier(jnp.sum(weights * picked, axis=2)).astype(jnp.bfloat16)

def reference(prompt_hidden, decode_hidden, norm_gain, w_dkv, kv_gain, w_gate, w_up, w_down, expert_ids, gate_values, owner, prompt_lengths, context_lengths):
    pnormed = rms_scale(prompt_hidden.astype(jnp.float32), norm_gain).astype(jnp.bfloat16)
    pcomp = jnp.dot(pnormed.reshape(-1, D), w_dkv, preferred_element_type=jnp.float32)
    pcomp = pcomp.reshape(N_HALF, N_SEQ, N_EXP, ROWS, LATW)
    row = jnp.arange(ROWS).astype(jnp.int32)
    ppos = (jnp.arange(N_EXP).astype(jnp.int32) % SPAN)[:, None] * ROWS + row[None, :]
    platents = make_latents(pcomp, jnp.broadcast_to(ppos, (N_HALF, N_SEQ, N_EXP, ROWS)), kv_gain)
    lens = jnp.repeat(prompt_lengths.reshape(N_HALF, N_SEQ, PGROUPS), SPAN, axis=2)
    keep = ppos[None, None] < lens[..., None]
    masked = jnp.where(keep[..., None], platents, jnp.zeros_like(platents)).reshape(OWNERS, N_EXP, ROWS, LATW)
    group_ids = jnp.broadcast_to(jnp.arange(OWNERS).astype(jnp.int32)[None, :], (PGROUPS, OWNERS))
    block_ids = jnp.arange(PGROUPS).astype(jnp.int32)[:, None]
    inverse = jnp.zeros((PGROUPS, OWNERS), jnp.int32).at[block_ids, owner].set(group_ids)
    source = inverse[jnp.arange(N_EXP).astype(jnp.int32) // SPAN].T
    owner_cache = masked[source, jnp.arange(N_EXP).astype(jnp.int32)[None, :]]
    owner_cache = owner_cache.reshape(N_HALF, N_SEQ, N_EXP, ROWS, LATW)
    dnormed = rms_scale(decode_hidden.astype(jnp.float32), norm_gain).astype(jnp.bfloat16)
    dcomp = jnp.dot(dnormed.reshape(-1, D), w_dkv, preferred_element_type=jnp.float32)
    dcomp = dcomp.reshape(N_HALF, N_SEQ, N_EXP, DROWS, LATW)
    drow = jnp.arange(DROWS).astype(jnp.int32)
    dpos = (jnp.repeat(context_lengths, 2, axis=-1) + drow % 2).astype(jnp.int32)
    new_latents = make_latents(dcomp, dpos, kv_gain)
    outputs = []
    for phase in range(N_HALF):
        tokens = dnormed[phase].reshape(N_SEQ * N_EXP, DROWS, D)
        ids = expert_ids[phase].reshape(N_SEQ * N_EXP, DROWS, TOP)
        gates = gate_values[phase].reshape(N_SEQ * N_EXP, DROWS, TOP)
        outputs.append(moe_half(tokens, ids, gates, w_gate, w_up, w_down).reshape(N_SEQ, N_EXP, DROWS, D))
    moe_out = jnp.stack(outputs)
    return (moe_out, new_latents, owner_cache)
```

```python
import functools

import jax
import jax.numpy as jnp
import numpy as np
from jax import lax
from jax.experimental import pallas as pl
from jax.experimental.pallas import tpu as pltpu
from jax.sharding import PartitionSpec as P

BF = jnp.bfloat16
F32 = jnp.float32
MESH = pl.DeviceIdType.MESH

D = 5120
LAT = 512
LATW = 576
FB = 192
ROWS = 256
DROWS = 4
TOP = 6
NS = 8
NE = 16
NG = 16
SLOTS = 256
DC = 4
DW = D // DC
META = 128
RC = 5
RW = D // RC
RQ = RW // 4

PLANE = (
    (0, 1), (1, 0), (0, 3), (3, 0), (1, 1), (3, 3), (1, 3), (3, 1),
    (0, 2), (2, 0), (1, 2), (2, 1), (3, 2), (2, 3), (2, 2),
)
ZOFF = (1, 7, 2, 6, 3, 5, 4)
COL = ((1, 0), (0, 1), (0, 7), (1, 1), (1, 7), (0, 2), (0, 6), (1, 2), (1, 6), (0, 3), (0, 5), (1, 3), (1, 5), (0, 4), (1, 4))

NT = (((1,), (1,)), ((), ()))


def iota(shape, dim):
    return lax.broadcasted_iota(jnp.int32, shape, dim)


def wait_bytes(ref, sem):
    pltpu.make_async_copy(ref, ref, sem).wait()


def latents(comp, pos, kv_gain, freq):
    lat = comp[:, :LAT]
    ms = jnp.mean(lat * lat, axis=-1, keepdims=True)
    lat = lat * lax.rsqrt(ms + 1e-06) * kv_gain
    rot = comp[:, LAT:]
    angle = pos * freq
    sine = jnp.sin(angle)
    swapped = jnp.concatenate([rot[:, 32:], rot[:, :32]], axis=-1)
    lane = iota(rot.shape, 1)
    rot = rot * jnp.cos(angle) + jnp.where(lane < 32, -sine, sine) * swapped
    return lat, rot


def kernel(
    dh, ng, kg, freq, ids, gates, owner, plen, ctx, ph_hbm, wk_hbm, wg_hbm, wu_hbm, wd_hbm,
    moe_out, newlat_out, cache_out,
    ph, wk, wgu, wd, xp, comp, msg, gath, sbuf, xbuf, hacc, actb, ybuf, rbuf, fbuf, qbuf, pbuf, abuf, bbuf, cbuf,
    lsem, zs, zr, ds_, dr, p1s, p1r, p2s, p2r, rs, rr, fs, fr,
):
    h = lax.axis_index("half")
    s = lax.axis_index("seq")
    e = lax.axis_index("exp")
    y = e // 4
    x = e % 4
    g = h * NS + s
    plane_ids = [((y + dy) % 4) * 4 + (x + dx) % 4 for dy, dx in PLANE]
    z_ids = [(s + d) % NS for d in ZOFF]
    col_ids = [((h + dh_) % 2, (s + d) % NS) for dh_, d in COL]

    barrier = pltpu.get_barrier_semaphore()
    for p in plane_ids:
        pl.semaphore_signal(barrier, inc=1, device_id=(h, s, p), device_id_type=MESH)
    for hp, sp in col_ids:
        pl.semaphore_signal(barrier, inc=1, device_id=(hp, sp, e), device_id_type=MESH)

    loads = [
        pltpu.make_async_copy(ph_hbm, ph, lsem.at[0]),
        pltpu.make_async_copy(wk_hbm, wk, lsem.at[1]),
        pltpu.make_async_copy(wg_hbm, wgu.at[pl.ds(0, FB)], lsem.at[2]),
        pltpu.make_async_copy(wu_hbm, wgu.at[pl.ds(FB, FB)], lsem.at[3]),
        pltpu.make_async_copy(wd_hbm, wd, lsem.at[4]),
    ]
    for c in loads:
        c.start()

    dec = dh[...].astype(F32)
    ms = jnp.mean(dec * dec, axis=-1, keepdims=True)
    dn = dec * lax.rsqrt(ms + 1e-06) * ng[...]
    msg[:, pl.ds(0, DW)] = jnp.concatenate([dn[:, q * DW:(q + 1) * DW] for q in range(4)], axis=0).astype(BF)
    xp[pl.ds(ROWS, 16), :] = jnp.concatenate([dn, jnp.zeros((12, D), F32)], axis=0).astype(BF)
    lane = iota((1, META), 1)
    kind = lane // 32
    xl = (lane % 32) // 2
    cl = lane % 2
    before = jnp.zeros((1, META), jnp.int32)
    rows = []
    for r in range(DROWS):
        named = jnp.zeros((1, META), jnp.int32)
        gv = jnp.zeros((1, META), F32)
        for k in range(TOP):
            hit = xl == ids[r, k]
            named = named + jnp.where(hit, 1, 0)
            gv = gv + jnp.where(hit, gates[r, k], 0.0)
        hi = gv.astype(BF).astype(F32)
        val = jnp.where(kind == 0, 1.0, jnp.where(kind == 1, hi, jnp.where(kind == 2, gv - hi, 0.0)))
        rows.append(jnp.where((named > 0) & (before == cl), val, 0.0))
        before = before + named
    meta4 = jnp.concatenate(rows, axis=0)
    msg[:, pl.ds(DW, META)] = jnp.concatenate([meta4] * 4, axis=0).astype(BF)

    pl.semaphore_wait(barrier, len(PLANE) + len(COL))

    my_rows = pl.ds(pl.multiple_of(s * 16, 16), 16)
    for p in z_ids:
        pltpu.make_async_remote_copy(msg, gath.at[my_rows], zs, zr, device_id=(h, p, e), device_id_type=MESH).start()
    gath[my_rows, :] = msg[...]

    loads[0].wait()

    def pnorm(i, _):
        at = pl.ds(pl.multiple_of(i * 32, 32), 32)
        v = ph[at, :].astype(F32)
        m = jnp.mean(v * v, axis=-1, keepdims=True)
        xp[at, :] = (v * lax.rsqrt(m + 1e-06) * ng[...]).astype(BF)
        return 0

    lax.fori_loop(0, ROWS // 32, pnorm, 0)

    wait_bytes(gath.at[pl.ds(0, 112)], zr)
    mt = gath[:, pl.ds(DW, META)]
    ei = iota((SLOTS, META), 0)
    ej = iota((SLOTS, META), 1)
    same = ((ei // 16) == ((ej % 32) // 2)) & ((ei % 2) == (ej % 2))
    et_slot = jnp.where(same & (ej // 32 == 0), 1.0, 0.0).astype(BF)
    et_gate = jnp.where(same & ((ej // 32 == 1) | (ej // 32 == 2)), 1.0, 0.0).astype(BF)
    t2 = lax.dot_general(et_slot, mt, NT, preferred_element_type=F32)
    samez = ((ei // 2) % 8) == (ej // 16)
    own = pl.ds(pl.multiple_of(e * 16, 16), 16)

    def dispatch(q, _):
        sel = jnp.where(samez & ((ej // 4) % 4 == q), t2, 0.0).astype(BF)
        sbuf[q] = jnp.dot(sel, gath[:, pl.ds(0, DW)], preferred_element_type=F32).astype(BF)
        for p in plane_ids:
            pltpu.make_async_remote_copy(
                sbuf.at[q, pl.ds(pl.multiple_of(p * 16, 16), 16)], xbuf.at[q, own], ds_.at[q], dr.at[q],
                device_id=(h, s, p), device_id_type=MESH).start()
        xbuf[q, own, :] = sbuf[q, own, :]
        return 0

    lax.fori_loop(0, DC, dispatch, 0)

    loads[1].wait()
    comp[...] = jnp.zeros_like(comp)

    def compress(i, _):
        at = pl.ds(pl.multiple_of(i * 1024, 1024), 1024)
        comp[...] += lax.dot_general(xp[:, at], wk[:, at], NT, preferred_element_type=F32)
        return 0

    lax.fori_loop(0, D // 1024, compress, 0)
    length = plen[g * NE + e]

    def prompt_latents(i, _):
        at = pl.ds(pl.multiple_of(i * 64, 64), 64)
        rid = iota((64, 1), 0) + i * 64
        lat, rot = latents(comp[at, :], rid.astype(F32), kg[...], freq[...])
        pbuf[at, pl.ds(0, LAT)] = jnp.where(rid < length, lat, 0.0).astype(BF)
        pbuf[at, pl.ds(LAT, 64)] = jnp.where(rid < length, rot, 0.0).astype(BF)
        return 0

    lax.fori_loop(0, ROWS // 64, prompt_latents, 0)
    mine = pl.ds(pl.multiple_of(g * 16, 16), 16)
    for hp, sp in col_ids:
        pltpu.make_async_remote_copy(
            pbuf.at[pl.ds(pl.multiple_of((hp * NS + sp) * 16, 16), 16)], abuf.at[mine], p1s, p1r,
            device_id=(hp, sp, e), device_id_type=MESH).start()
    abuf[mine, :] = pbuf[mine, :]

    rid = iota((16, 1), 0)
    dpos = jnp.where(rid < 2, ctx[0, 0], ctx[0, 1]) + rid % 2
    lat, rot = latents(comp[pl.ds(ROWS, 16), :], dpos.astype(F32), kg[...], freq[...])
    newlat_out[:, pl.ds(0, LAT)] = lat[:DROWS].astype(BF)
    newlat_out[:, pl.ds(LAT, 64)] = rot[:DROWS].astype(BF)

    lane = iota((1, ROWS), 1)
    to = jnp.zeros((1, ROWS), jnp.int32)
    for k in range(NG):
        to = to + jnp.where(lane // 16 == k, owner[e, k], 0)
    pi = iota((ROWS, ROWS), 0)
    pj = iota((ROWS, ROWS), 1)
    perm = jnp.where((pi // 16 == to) & (pi % 16 == pj % 16), 1.0, 0.0).astype(BF)
    wait_bytes(abuf.at[pl.ds(0, 240)], p1r)
    bbuf[...] = jnp.dot(perm, abuf[...], preferred_element_type=F32).astype(BF)
    for hp, sp in col_ids:
        pltpu.make_async_remote_copy(
            bbuf.at[pl.ds(pl.multiple_of((hp * NS + sp) * 16, 16), 16)], cbuf.at[mine], p2s, p2r,
            device_id=(hp, sp, e), device_id_type=MESH).start()
    cbuf[mine, :] = bbuf[mine, :]

    loads[2].wait()
    loads[3].wait()
    hacc[...] = jnp.zeros_like(hacc)

    def up(q, _):
        wait_bytes(xbuf.at[q, pl.ds(0, 240)], dr.at[q])
        at = pl.ds(pl.multiple_of(q * DW, DW), DW)
        hacc[...] += lax.dot_general(xbuf[q], wgu[:, at], NT, preferred_element_type=F32)
        return 0

    lax.fori_loop(0, DC, up, 0)
    gate = hacc[:, pl.ds(0, FB)]
    actb[...] = (gate * jax.nn.sigmoid(gate) * hacc[:, pl.ds(FB, FB)]).astype(BF)
    loads[4].wait()

    def down(k, _):
        at = pl.ds(pl.multiple_of(k * RW, RW), RW)
        ybuf[k] = jnp.dot(actb[...], wd[:, at], preferred_element_type=F32).astype(BF)
        for p in plane_ids:
            pltpu.make_async_remote_copy(
                ybuf.at[k, pl.ds(pl.multiple_of(p * 16, 16), 16)], rbuf.at[k, own], rs.at[k], rr.at[k],
                device_id=(h, s, p), device_id_type=MESH).start()
        rbuf[k, own, :] = ybuf[k, own, :]
        return 0

    lax.fori_loop(0, RC, down, 0)

    wait_bytes(cbuf.at[pl.ds(0, 240)], p2r)
    cache_out[...] = cbuf[...].astype(F32).T.astype(BF)

    cg = lax.dot_general(gath[:, pl.ds(DW, META)], et_gate, NT, preferred_element_type=F32)
    ci = iota((META, SLOTS), 0)
    cj = iota((META, SLOTS), 1)
    cz = (ci // 16) == ((cj // 2) % 8)

    def combine(k, _):
        wait_bytes(rbuf.at[k, pl.ds(0, 240)], rr.at[k])
        total = jnp.zeros((META, RQ), F32)
        for q in range(4):
            w = jnp.where(cz & ((ci // 4) % 4 == q), cg, 0.0)
            hi = w.astype(BF)
            lo = (w - hi.astype(F32)).astype(BF)
            part = rbuf[k, :, pl.ds(q * RQ, RQ)]
            total += jnp.dot(hi, part, preferred_element_type=F32)
            total += jnp.dot(lo, part, preferred_element_type=F32)
        fbuf[k] = total.astype(BF)
        for p in z_ids:
            pltpu.make_async_remote_copy(
                fbuf.at[k, pl.ds(pl.multiple_of(p * 16, 16), 16)], qbuf.at[k, my_rows], fs.at[k], fr.at[k],
                device_id=(h, p, e), device_id_type=MESH).start()
        qbuf[k, my_rows, :] = fbuf[k, my_rows, :]
        return 0

    lax.fori_loop(0, RC, combine, 0)

    for k in range(RC):
        wait_bytes(qbuf.at[k, pl.ds(0, 112)], fr.at[k])
        tot = jnp.zeros((16, RQ), F32)
        for z in range(NS):
            tot += qbuf[k, pl.ds(z * 16, 16), :].astype(F32)
        for q in range(4):
            moe_out[:, pl.ds(k * RW + q * RQ, RQ)] = tot[q * 4:q * 4 + 4, :].astype(BF)

    for k in range(RC):
        wait_bytes(fbuf.at[k, pl.ds(0, 112)], fs.at[k])
        wait_bytes(ybuf.at[k, pl.ds(0, 240)], rs.at[k])
    for q in range(DC):
        wait_bytes(sbuf.at[q, pl.ds(0, 240)], ds_.at[q])
    wait_bytes(gath.at[pl.ds(0, 112)], zs)
    wait_bytes(pbuf.at[pl.ds(0, 240)], p1s)
    wait_bytes(bbuf.at[pl.ds(0, 240)], p2s)


def shards(
    prompt_hidden, decode_hidden, norm_gain, w_dkv, kv_gain, w_gate, w_up, w_down, expert_ids, gate_values,
    owner, prompt_lengths, context_lengths,
):
    freq = 10000.0 ** (-(np.arange(32, dtype=np.float64) * 2.0 / 64))
    freq = jnp.asarray(np.concatenate([freq, freq])[None, :], F32)
    vm = pl.BlockSpec(memory_space=pltpu.VMEM)
    sm = pl.BlockSpec(memory_space=pltpu.SMEM)
    hbm = pl.BlockSpec(memory_space=pl.ANY)
    dma = pltpu.SemaphoreType.DMA
    moe, newlat, cache = pl.pallas_call(
        kernel,
        out_shape=(
            jax.ShapeDtypeStruct((DROWS, D), BF),
            jax.ShapeDtypeStruct((DROWS, LATW), BF),
            jax.ShapeDtypeStruct((LATW, ROWS), BF),
        ),
        in_specs=[vm] * 4 + [sm] * 5 + [hbm] * 5,
        out_specs=(vm, vm, vm),
        scratch_shapes=[
            pltpu.VMEM((ROWS, D), BF),
            pltpu.VMEM((LATW, D), BF),
            pltpu.VMEM((2 * FB, D), BF),
            pltpu.VMEM((FB, D), BF),
            pltpu.VMEM((ROWS + 16, D), BF),
            pltpu.VMEM((ROWS + 16, LATW), F32),
            pltpu.VMEM((16, DW + META), BF),
            pltpu.VMEM((NS * 16, DW + META), BF),
            pltpu.VMEM((DC, SLOTS, DW), BF),
            pltpu.VMEM((DC, SLOTS, DW), BF),
            pltpu.VMEM((SLOTS, 2 * FB), F32),
            pltpu.VMEM((SLOTS, FB), BF),
            pltpu.VMEM((RC, SLOTS, RW), BF),
            pltpu.VMEM((RC, SLOTS, RW), BF),
            pltpu.VMEM((RC, NS * 16, RQ), BF),
            pltpu.VMEM((RC, NS * 16, RQ), BF),
            pltpu.VMEM((ROWS, LATW), BF),
            pltpu.VMEM((ROWS, LATW), BF),
            pltpu.VMEM((ROWS, LATW), BF),
            pltpu.VMEM((ROWS, LATW), BF),
            dma((5,)), dma, dma, dma((DC,)), dma((DC,)), dma, dma, dma, dma, dma((RC,)), dma((RC,)), dma((RC,)), dma((RC,)),
        ],
        compiler_params=pltpu.CompilerParams(collective_id=0, has_side_effects=True, vmem_limit_bytes=56 * 2**20),
        cost_estimate=pl.CostEstimate(flops=4 * 10**9, bytes_accessed=16 * 10**6, transcendentals=10**5),
        name="layer_slice",
    )(
        decode_hidden.reshape(DROWS, D), norm_gain.reshape(1, D), kv_gain.reshape(1, LAT), freq,
        expert_ids.reshape(DROWS, TOP), gate_values.reshape(DROWS, TOP), owner, prompt_lengths,
        context_lengths.reshape(1, 2),
        prompt_hidden.reshape(ROWS, D), w_dkv.T, w_gate[0].T, w_up[0].T, w_down[0],
    )
    return (
        moe.reshape(1, 1, 1, DROWS, D),
        newlat.reshape(1, 1, 1, DROWS, LATW),
        cache.T.reshape(1, 1, 1, ROWS, LATW),
    )


def solution(mesh):
    token = P("half", "seq", "exp", None, None)
    in_specs = (
        token, token, P(), P(), P(), P("exp", None, "seq"), P("exp", None, "seq"), P("exp", "seq", None),
        token, token, P(), P(), P("half", "seq", "exp", None),
    )
    return jax.shard_map(shards, mesh=mesh, in_specs=in_specs, out_specs=(token, token, token), check_vma=False)
```

```python
import functools

import jax
import jax.numpy as jnp
import numpy as np
from jax import lax
from jax.experimental import pallas as pl
from jax.experimental.pallas import tpu as pltpu
from jax.sharding import PartitionSpec as P

BF = jnp.bfloat16
F32 = jnp.float32
MESH = pl.DeviceIdType.MESH

D = 5120
LAT = 512
LATW = 576
FB = 192
ROWS = 256
DROWS = 4
TOP = 6
NS = 8
NE = 16
NG = 16
SLOTS = 256
CZ = 3072
CP = D - CZ
HP = CP // 2
DC = 4
DW = CZ // DC
MW = CZ // 8
META = 128
RC = 3
RW = CZ // RC
RQ = RW // 4
PQ = 8
PW = CP // PQ

PLANE = (
    (0, 1), (1, 0), (0, 3), (3, 0), (1, 1), (3, 3), (1, 3), (3, 1),
    (0, 2), (2, 0), (1, 2), (2, 1), (3, 2), (2, 3), (2, 2),
)
ZOFF = (4, 3, 5, 2, 6, 1, 7)
COL = ((1, 0), (0, 1), (0, 7), (1, 1), (1, 7), (0, 2), (0, 6), (1, 2), (1, 6), (0, 3), (0, 5), (1, 3), (1, 5), (0, 4), (1, 4))

NT = (((1,), (1,)), ((), ()))


def iota(shape, dim):
    return lax.broadcasted_iota(jnp.int32, shape, dim)


def wait_bytes(ref, sem):
    pltpu.make_async_copy(ref, ref, sem).wait()


def latents(comp, pos, kv_gain, freq):
    lat = comp[:, :LAT]
    ms = jnp.mean(lat * lat, axis=-1, keepdims=True)
    lat = lat * lax.rsqrt(ms + 1e-06) * kv_gain
    rot = comp[:, LAT:]
    angle = pos * freq
    sine = jnp.sin(angle)
    swapped = jnp.concatenate([rot[:, 32:], rot[:, :32]], axis=-1)
    lane = iota(rot.shape, 1)
    rot = rot * jnp.cos(angle) + jnp.where(lane < 32, -sine, sine) * swapped
    return lat, rot


def kernel(
    dh, ng, kg, freq, ids, gates, owner, plen, ctx, ph_hbm, wk_hbm, wg_hbm, wu_hbm, wd_hbm,
    moe_out, newlat_out, cache_out,
    ph, wk, wgu, wd, xp, comp, msg, gath, sbuf, xbuf, hacc, actb, ybuf, rbuf, fbuf, qbuf, pbuf, abuf, bbuf, cbuf,
    mtp, pmsg, parr, pxb, ypb, sumr, suml, gotr, gotl, pfold, pback, wts,
    lsem, zs, zr, ds_, dr, p1s, p1r, p2s, p2r, rs, rr, fs, fr,
    ps, pr, gs, gr, us, ur, bs, br,
):
    h = lax.axis_index("half")
    s = lax.axis_index("seq")
    e = lax.axis_index("exp")
    y = e // 4
    x = e % 4
    g = h * NS + s
    plane_ids = [((y + dy) % 4) * 4 + (x + dx) % 4 for dy, dx in PLANE]
    z_ids = [(s + d) % NS for d in ZOFF]
    col_ids = [((h + dh_) % 2, (s + d) % NS) for dh_, d in COL]

    barrier = pltpu.get_barrier_semaphore()
    for p in plane_ids:
        pl.semaphore_signal(barrier, inc=1, device_id=(h, s, p), device_id_type=MESH)
    for hp, sp in col_ids:
        pl.semaphore_signal(barrier, inc=1, device_id=(hp, sp, e), device_id_type=MESH)

    loads = [
        pltpu.make_async_copy(ph_hbm, ph, lsem.at[0]),
        pltpu.make_async_copy(wk_hbm, wk, lsem.at[1]),
        pltpu.make_async_copy(wg_hbm, wgu.at[pl.ds(0, FB)], lsem.at[2]),
        pltpu.make_async_copy(wu_hbm, wgu.at[pl.ds(FB, FB)], lsem.at[3]),
        pltpu.make_async_copy(wd_hbm, wd, lsem.at[4]),
    ]
    for c in loads:
        c.start()

    dec = dh[...].astype(F32)
    ms = jnp.mean(dec * dec, axis=-1, keepdims=True)
    dn = dec * lax.rsqrt(ms + 1e-06) * ng[...]
    for i, at in enumerate((0, MW + META)):
        msg[:, pl.ds(at, MW)] = jnp.concatenate(
            [dn[:, (4 * i + q) * MW:(4 * i + q + 1) * MW] for q in range(4)], axis=0).astype(BF)
    xp[pl.ds(ROWS, 16), :] = jnp.concatenate([dn, jnp.zeros((12, D), F32)], axis=0).astype(BF)
    lane = iota((1, META), 1)
    kind = lane // 32
    xl = (lane % 32) // 2
    cl = lane % 2
    before = jnp.zeros((1, META), jnp.int32)
    rows = []
    for r in range(DROWS):
        named = jnp.zeros((1, META), jnp.int32)
        gv = jnp.zeros((1, META), F32)
        for k in range(TOP):
            hit = xl == ids[r, k]
            named = named + jnp.where(hit, 1, 0)
            gv = gv + jnp.where(hit, gates[r, k], 0.0)
        hi = gv.astype(BF).astype(F32)
        val = jnp.where(kind == 0, 1.0, jnp.where(kind == 1, hi, jnp.where(kind == 2, gv - hi, 0.0)))
        rows.append(jnp.where((named > 0) & (before == cl), val, 0.0))
        before = before + named
    meta4 = jnp.concatenate(rows, axis=0)
    msg[:, pl.ds(MW, META)] = jnp.concatenate([meta4] * 4, axis=0).astype(BF)

    mtp[...] = jnp.concatenate([meta4] * PQ, axis=0).astype(BF)
    fi = iota((SLOTS, META), 0)
    fj = iota((SLOTS, META), 1)
    fsame = ((fi // 16) == ((fj % 32) // 2)) & (((fi // 8) % 2) == (fj % 2))
    fold_slot = jnp.where(fsame & (fj // 32 == 0), 1.0, 0.0).astype(BF)
    tf = lax.dot_general(fold_slot, mtp[...], NT, preferred_element_type=F32)
    self_ = jnp.where(iota((SLOTS, 4 * PQ), 0) % PQ == iota((SLOTS, 4 * PQ), 1) // 4, tf, 0.0).astype(BF)
    dcols = jnp.concatenate([dn[:, CZ + q * PW:CZ + (q + 1) * PW] for q in range(PQ)], axis=0).astype(BF)
    pmsg[...] = jnp.dot(self_, dcols, preferred_element_type=F32).astype(BF)

    pl.semaphore_wait(barrier, len(PLANE) + len(COL))

    my_rows = pl.ds(pl.multiple_of(s * 16, 16), 16)
    own = pl.ds(pl.multiple_of(e * 16, 16), 16)
    pieces = (pl.ds(0, MW + META), pl.ds(MW + META, MW))
    for i, cols in enumerate(pieces):
        for p in z_ids:
            pltpu.make_async_remote_copy(
                msg.at[:, cols], gath.at[my_rows, cols], zs.at[i], zr.at[i], device_id=(h, p, e), device_id_type=MESH).start()
    for p in plane_ids:
        pltpu.make_async_remote_copy(
            pmsg.at[pl.ds(pl.multiple_of(p * 16, 16), 16)], parr.at[own], ps, pr,
            device_id=(h, s, p), device_id_type=MESH).start()
    gath[my_rows, :] = msg[...]
    parr[own, :] = pmsg[own, :]

    loads[0].wait()

    def pnorm(i, _):
        at = pl.ds(pl.multiple_of(i * 32, 32), 32)
        v = ph[at, :].astype(F32)
        m = jnp.mean(v * v, axis=-1, keepdims=True)
        xp[at, :] = (v * lax.rsqrt(m + 1e-06) * ng[...]).astype(BF)
        return 0

    lax.fori_loop(0, ROWS // 32, pnorm, 0)

    right = (s + 1) % NS
    left = (s + 7) % NS

    sides = (right, left)
    halves = (pl.ds(0, HP), pl.ds(HP, HP))

    def block(d, t):
        return (s + NS - t) % NS if d == 0 else (s + t) % NS

    def gather_send(d, t, u):
        if t > 0:
            wait_bytes(pxb.at[block(d, t), :, halves[u]], gr.at[d, t - 1, u])
        part = pxb.at[block(d, t), :, halves[u]]
        pltpu.make_async_remote_copy(
            part, part, gs.at[d, t, u], gr.at[d, t, u], device_id=(h, sides[d], e), device_id_type=MESH).start()

    def gather_step(t):
        for d in range(2):
            gather_send(d, t, d)
        if t < 3:
            for d in range(2):
                gather_send(d, t, 1 - d)

    def gather_end():
        for d in range(2):
            wait_bytes(pxb.at[block(d, 4), :, halves[d]], gr.at[d, 3, d])
            wait_bytes(pxb.at[block(d, 3), :, halves[1 - d]], gr.at[d, 2, 1 - d])

    ui = iota((SLOTS, SLOTS), 0)
    uj = iota((SLOTS, SLOTS), 1)
    unfold = jnp.where(uj == ((ui % 32) // 2) * 16 + (ui % 2) * 8 + ui // 32, 1.0, 0.0).astype(BF)
    wait_bytes(parr.at[pl.ds(0, 240)], pr)
    flat = jnp.dot(unfold, parr[...], preferred_element_type=F32).astype(BF)
    for q in range(PQ):
        pxb[s, :, pl.ds(q * PW, PW)] = flat[q * 32:(q + 1) * 32, :]
    gather_step(0)

    loads[1].wait()
    comp[...] = jnp.zeros_like(comp)

    def compress(i, _):
        at = pl.ds(pl.multiple_of(i * 1024, 1024), 1024)
        comp[...] += lax.dot_general(xp[:, at], wk[:, at], NT, preferred_element_type=F32)
        return 0

    lax.fori_loop(0, D // 1024, compress, 0)
    length = plen[g * NE + e]

    def prompt_latents(i, _):
        at = pl.ds(pl.multiple_of(i * 64, 64), 64)
        rid = iota((64, 1), 0) + i * 64
        lat, rot = latents(comp[at, :], rid.astype(F32), kg[...], freq[...])
        pbuf[at, pl.ds(0, LAT)] = jnp.where(rid < length, lat, 0.0).astype(BF)
        pbuf[at, pl.ds(LAT, 64)] = jnp.where(rid < length, rot, 0.0).astype(BF)
        return 0

    lax.fori_loop(0, ROWS // 64, prompt_latents, 0)
    mine = pl.ds(pl.multiple_of(g * 16, 16), 16)
    for hp, sp in col_ids:
        pltpu.make_async_remote_copy(
            pbuf.at[pl.ds(pl.multiple_of((hp * NS + sp) * 16, 16), 16)], abuf.at[mine], p1s, p1r,
            device_id=(hp, sp, e), device_id_type=MESH).start()
    abuf[mine, :] = pbuf[mine, :]


    wait_bytes(gath.at[pl.ds(0, 112), pieces[0]], zr.at[0])
    mt = gath[:, pl.ds(MW, META)]
    ei = iota((SLOTS, META), 0)
    ej = iota((SLOTS, META), 1)
    same = ((ei // 16) == ((ej % 32) // 2)) & ((ei % 2) == (ej % 2))
    et_slot = jnp.where(same & (ej // 32 == 0), 1.0, 0.0).astype(BF)
    et_gate = jnp.where(same & ((ej // 32 == 1) | (ej // 32 == 2)), 1.0, 0.0).astype(BF)
    t2 = lax.dot_general(et_slot, mt, NT, preferred_element_type=F32)
    samez = ((ei // 2) % 8) == (ej // 16)

    selects = [jnp.where(samez & ((ej // 4) % 4 == q), t2, 0.0).astype(BF) for q in range(4)]

    def dispatch(c):
        if c == 2:
            wait_bytes(gath.at[pl.ds(0, 112), pieces[1]], zr.at[1])
        cols = gath[:, pl.ds((c // 2) * (MW + META), MW)]
        for j in range(2):
            sbuf[c, :, pl.ds(j * MW, MW)] = jnp.dot(
                selects[(c % 2) * 2 + j], cols, preferred_element_type=F32).astype(BF)
        for p in plane_ids:
            pltpu.make_async_remote_copy(
                sbuf.at[c, pl.ds(pl.multiple_of(p * 16, 16), 16)], xbuf.at[c, own], ds_.at[c], dr.at[c],
                device_id=(h, s, p), device_id_type=MESH).start()
        xbuf[c, own, :] = sbuf[c, own, :]

    dispatch(0)
    dispatch(1)
    gather_step(1)
    dispatch(2)
    dispatch(3)
    gather_step(2)

    cg = lax.dot_general(mt, et_gate, NT, preferred_element_type=F32)
    ci = iota((META, SLOTS), 0)
    cj = iota((META, SLOTS), 1)
    cz = (ci // 16) == ((cj // 2) % 8)
    for q in range(4):
        w = jnp.where(cz & ((ci // 4) % 4 == q), cg, 0.0)
        hi = w.astype(BF)
        wts[q] = hi
        wts[q + 4] = (w - hi.astype(F32)).astype(BF)
    rid = iota((16, 1), 0)
    dpos = jnp.where(rid < 2, ctx[0, 0], ctx[0, 1]) + rid % 2
    lat, rot = latents(comp[pl.ds(ROWS, 16), :], dpos.astype(F32), kg[...], freq[...])
    newlat_out[:, pl.ds(0, LAT)] = lat[:DROWS].astype(BF)
    newlat_out[:, pl.ds(LAT, 64)] = rot[:DROWS].astype(BF)

    gather_step(3)

    lane = iota((1, ROWS), 1)
    to = jnp.zeros((1, ROWS), jnp.int32)
    for k in range(NG):
        to = to + jnp.where(lane // 16 == k, owner[e, k], 0)
    pi = iota((ROWS, ROWS), 0)
    pj = iota((ROWS, ROWS), 1)
    perm = jnp.where((pi // 16 == to) & (pi % 16 == pj % 16), 1.0, 0.0).astype(BF)
    loads[2].wait()
    loads[3].wait()
    hacc[...] = jnp.zeros_like(hacc)

    def up(q, _):
        wait_bytes(xbuf.at[q, pl.ds(0, 240)], dr.at[q])
        at = pl.ds(pl.multiple_of(q * DW, DW), DW)
        hacc[...] += lax.dot_general(xbuf[q], wgu[:, at], NT, preferred_element_type=F32)
        return 0

    lax.fori_loop(0, DC - 1, up, 0)
    gather_end()
    order = jnp.where(
        ((ui // 16) == ((uj % 32) // 2)) & (((ui // 2) % 8) == uj // 32) & ((ui % 2) == (uj % 2)), 1.0, 0.0).astype(BF)
    back = jnp.where(
        ((uj // 16) == ((ui % 32) // 2)) & (((uj // 2) % 8) == ui // 32) & ((uj % 2) == (ui % 2)), 1.0, 0.0).astype(BF)
    hp_ = lax.dot_general(pxb[...].reshape(SLOTS, CP), wgu[:, pl.ds(CZ, CP)], NT, preferred_element_type=F32)
    hp_hi = hp_.astype(BF)
    hp_lo = (hp_ - hp_hi.astype(F32)).astype(BF)
    hacc[...] += jnp.dot(order, hp_hi, preferred_element_type=F32) + jnp.dot(order, hp_lo, preferred_element_type=F32)
    wait_bytes(abuf.at[pl.ds(0, 240)], p1r)
    bbuf[...] = jnp.dot(perm, abuf[...], preferred_element_type=F32).astype(BF)
    for hp, sp in col_ids:
        pltpu.make_async_remote_copy(
            bbuf.at[pl.ds(pl.multiple_of((hp * NS + sp) * 16, 16), 16)], cbuf.at[mine], p2s, p2r,
            device_id=(hp, sp, e), device_id_type=MESH).start()
    cbuf[mine, :] = bbuf[mine, :]

    up(DC - 1, 0)
    gate = hacc[:, pl.ds(0, FB)]
    actb[...] = (gate * jax.nn.sigmoid(gate) * hacc[:, pl.ds(FB, FB)]).astype(BF)
    loads[4].wait()

    def down(k, _):
        at = pl.ds(pl.multiple_of(k * RW, RW), RW)
        ybuf[k] = jnp.dot(actb[...], wd[:, at], preferred_element_type=F32).astype(BF)
        for p in plane_ids:
            pltpu.make_async_remote_copy(
                ybuf.at[k, pl.ds(pl.multiple_of(p * 16, 16), 16)], rbuf.at[k, own], rs.at[k], rr.at[k],
                device_id=(h, s, p), device_id_type=MESH).start()
        rbuf[k, own, :] = ybuf[k, own, :]
        return 0

    down(0, 0)

    actp = jnp.dot(back, actb[...], preferred_element_type=F32).astype(BF)
    ypb[...] = jnp.dot(actp, wd[:, pl.ds(CZ, CP)], preferred_element_type=F32).astype(BF).reshape(NS, 32, CP)
    got = (gotr, gotl)
    summed = (sumr, suml)

    def sum_send(d, t, u):
        dest = (s + 4 - t) % NS if d == 0 else (s + 4 + t) % NS
        at = halves[u]
        if t == (0 if u == d else 1):
            src = ypb.at[dest, :, at]
        else:
            wait_bytes(got[d].at[t - 1, :, at], ur.at[d, t - 1, u])
            summed[d][t - 1, :, at] = (ypb[dest, :, at].astype(F32) + got[d][t - 1, :, at].astype(F32)).astype(BF)
            src = summed[d].at[t - 1, :, at]
        pltpu.make_async_remote_copy(
            src, got[d].at[t, :, at], us.at[d, t, u], ur.at[d, t, u],
            device_id=(h, sides[d], e), device_id_type=MESH).start()

    for d in range(2):
        sum_send(d, 0, d)
    for d in range(2):
        sum_send(d, 1, 1 - d)
    for k in range(1, RC):
        down(k, 0)

    def sum_step(t):
        for d in range(2):
            sum_send(d, t, d)
        if t < 3:
            for d in range(2):
                sum_send(d, t + 1, 1 - d)


    def combine(k, _):
        wait_bytes(rbuf.at[k, pl.ds(0, 240)], rr.at[k])
        total = jnp.zeros((META, RQ), F32)
        for q in range(4):
            part = rbuf[k, :, pl.ds(q * RQ, RQ)]
            total += jnp.dot(wts[q], part, preferred_element_type=F32)
            total += jnp.dot(wts[q + 4], part, preferred_element_type=F32)
        fbuf[k] = total.astype(BF)
        for p in z_ids:
            pltpu.make_async_remote_copy(
                fbuf.at[k, pl.ds(pl.multiple_of(p * 16, 16), 16)], qbuf.at[k, my_rows], fs.at[k], fr.at[k],
                device_id=(h, p, e), device_id_type=MESH).start()
        qbuf[k, my_rows, :] = fbuf[k, my_rows, :]
        return 0

    sum_step(1)
    sum_step(2)
    for k in range(RC - 2):
        combine(k, 0)
    sum_step(3)
    for k in range(RC - 2, RC):
        combine(k, 0)
    for d in range(2):
        for u in range(2):
            wait_bytes(got[d].at[3, :, halves[u]], ur.at[d, 3, u])
    done = (ypb[s].astype(F32) + gotr[3].astype(F32) + gotl[3].astype(F32)).astype(BF)
    stacked = jnp.concatenate([done[:, q * PW:(q + 1) * PW] for q in range(PQ)], axis=0)
    refold = jnp.where(ui == ((uj % 32) // 2) * 16 + (uj % 2) * 8 + uj // 32, 1.0, 0.0).astype(BF)
    pfold[...] = jnp.dot(refold, stacked, preferred_element_type=F32).astype(BF)
    for p in plane_ids:
        pltpu.make_async_remote_copy(
            pfold.at[pl.ds(pl.multiple_of(p * 16, 16), 16)], pback.at[own], bs, br,
            device_id=(h, s, p), device_id_type=MESH).start()
    pback[own, :] = pfold[own, :]
    wait_bytes(cbuf.at[pl.ds(0, 240)], p2r)
    cache_out[...] = cbuf[...].astype(F32).T.astype(BF)


    fold_gate = jnp.where(fsame & ((fj // 32 == 1) | (fj // 32 == 2)), 1.0, 0.0).astype(BF)
    cp = lax.dot_general(mtp[...], fold_gate, NT, preferred_element_type=F32)
    cp = jnp.where(iota((4 * PQ, SLOTS), 1) % PQ == iota((4 * PQ, SLOTS), 0) // 4, cp, 0.0)
    cp_hi = cp.astype(BF)
    cp_lo = (cp - cp_hi.astype(F32)).astype(BF)
    wait_bytes(pback.at[pl.ds(0, 240)], br)
    ptot = jnp.dot(cp_hi, pback[...], preferred_element_type=F32) + jnp.dot(cp_lo, pback[...], preferred_element_type=F32)
    for q in range(PQ):
        moe_out[:, pl.ds(CZ + q * PW, PW)] = ptot[q * 4:q * 4 + 4, :].astype(BF)

    for k in range(RC):
        wait_bytes(qbuf.at[k, pl.ds(0, 112)], fr.at[k])
        tot = jnp.zeros((16, RQ), F32)
        for z in range(NS):
            tot += qbuf[k, pl.ds(z * 16, 16), :].astype(F32)
        for q in range(4):
            moe_out[:, pl.ds(k * RW + q * RQ, RQ)] = tot[q * 4:q * 4 + 4, :].astype(BF)

    for k in range(RC):
        wait_bytes(fbuf.at[k, pl.ds(0, 112)], fs.at[k])
        wait_bytes(ybuf.at[k, pl.ds(0, 240)], rs.at[k])
    for q in range(DC):
        wait_bytes(sbuf.at[q, pl.ds(0, 240)], ds_.at[q])
    for i, cols in enumerate(pieces):
        wait_bytes(gath.at[pl.ds(0, 112), cols], zs.at[i])
    wait_bytes(parr.at[pl.ds(0, 240)], ps)
    wait_bytes(pback.at[pl.ds(0, 240)], bs)
    for d in range(2):
        for u in range(2):
            for t in range(4):
                if u == d or t < 3:
                    wait_bytes(pxb.at[0, :, halves[u]], gs.at[d, t, u])
                if u == d or t > 0:
                    wait_bytes(ypb.at[0, :, halves[u]], us.at[d, t, u])
    wait_bytes(pbuf.at[pl.ds(0, 240)], p1s)
    wait_bytes(bbuf.at[pl.ds(0, 240)], p2s)


def finish(a, b, c, oa, ob, oc):
    oa[...] = a[...]
    ob[...] = b[...]
    oc[...] = c[...]


def shards(
    prompt_hidden, decode_hidden, norm_gain, w_dkv, kv_gain, w_gate, w_up, w_down, expert_ids, gate_values,
    owner, prompt_lengths, context_lengths,
):
    freq = 10000.0 ** (-(np.arange(32, dtype=np.float64) * 2.0 / 64))
    freq = jnp.asarray(np.concatenate([freq, freq])[None, :], F32)
    vm = pl.BlockSpec(memory_space=pltpu.VMEM)
    sm = pl.BlockSpec(memory_space=pltpu.SMEM)
    hbm = pl.BlockSpec(memory_space=pl.ANY)
    dma = pltpu.SemaphoreType.DMA
    moe, newlat, cache = pl.pallas_call(
        kernel,
        out_shape=(
            jax.ShapeDtypeStruct((DROWS, D), BF),
            jax.ShapeDtypeStruct((DROWS, LATW), BF),
            jax.ShapeDtypeStruct((LATW, ROWS), BF),
        ),
        in_specs=[vm] * 4 + [sm] * 5 + [hbm] * 5,
        out_specs=(vm, vm, vm),
        scratch_shapes=[
            pltpu.VMEM((ROWS, D), BF),
            pltpu.VMEM((LATW, D), BF),
            pltpu.VMEM((2 * FB, D), BF),
            pltpu.VMEM((FB, D), BF),
            pltpu.VMEM((ROWS + 16, D), BF),
            pltpu.VMEM((ROWS + 16, LATW), F32),
            pltpu.VMEM((16, 2 * MW + META), BF),
            pltpu.VMEM((NS * 16, 2 * MW + META), BF),
            pltpu.VMEM((DC, SLOTS, DW), BF),
            pltpu.VMEM((DC, SLOTS, DW), BF),
            pltpu.VMEM((SLOTS, 2 * FB), F32),
            pltpu.VMEM((SLOTS, FB), BF),
            pltpu.VMEM((RC, SLOTS, RW), BF),
            pltpu.VMEM((RC, SLOTS, RW), BF),
            pltpu.VMEM((RC, NS * 16, RQ), BF),
            pltpu.VMEM((RC, NS * 16, RQ), BF),
            pltpu.VMEM((ROWS, LATW), BF),
            pltpu.VMEM((ROWS, LATW), BF),
            pltpu.VMEM((ROWS, LATW), BF),
            pltpu.VMEM((ROWS, LATW), BF),
            pltpu.VMEM((4 * PQ, META), BF),
            pltpu.VMEM((SLOTS, PW), BF),
            pltpu.VMEM((SLOTS, PW), BF),
            pltpu.VMEM((NS, 32, CP), BF),
            pltpu.VMEM((NS, 32, CP), BF),
            pltpu.VMEM((3, 32, CP), BF),
            pltpu.VMEM((3, 32, CP), BF),
            pltpu.VMEM((4, 32, CP), BF),
            pltpu.VMEM((4, 32, CP), BF),
            pltpu.VMEM((SLOTS, PW), BF),
            pltpu.VMEM((SLOTS, PW), BF),
            pltpu.VMEM((8, META, SLOTS), BF),
            dma((5,)), dma((2,)), dma((2,)), dma((DC,)), dma((DC,)), dma, dma, dma, dma, dma((RC,)), dma((RC,)), dma((RC,)), dma((RC,)),
            dma, dma, dma((2, 4, 2)), dma((2, 4, 2)), dma((2, 4, 2)), dma((2, 4, 2)), dma, dma,
        ],
        compiler_params=pltpu.CompilerParams(collective_id=0, has_side_effects=True, vmem_limit_bytes=56 * 2**20),
        cost_estimate=pl.CostEstimate(flops=4 * 10**9, bytes_accessed=16 * 10**6, transcendentals=10**5),
        name="layer_slice",
    )(
        decode_hidden.reshape(DROWS, D), norm_gain.reshape(1, D), kv_gain.reshape(1, LAT), freq,
        expert_ids.reshape(DROWS, TOP), gate_values.reshape(DROWS, TOP), owner, prompt_lengths,
        context_lengths.reshape(1, 2),
        prompt_hidden.reshape(ROWS, D), w_dkv.T, w_gate[0].T, w_up[0].T, w_down[0],
    )
    moe, newlat, cache = pl.pallas_call(
        finish,
        out_shape=tuple(jax.ShapeDtypeStruct(v.shape, v.dtype) for v in (moe, newlat, cache)),
        in_specs=[vm] * 3,
        out_specs=(vm,) * 3,
        name="results",
    )(moe, newlat, cache)
    return (
        moe.reshape(1, 1, 1, DROWS, D),
        newlat.reshape(1, 1, 1, DROWS, LATW),
        cache.T.reshape(1, 1, 1, ROWS, LATW),
    )


def solution(mesh):
    token = P("half", "seq", "exp", None, None)
    in_specs = (
        token, token, P(), P(), P(), P("exp", None, "seq"), P("exp", None, "seq"), P("exp", "seq", None),
        token, token, P(), P(), P("half", "seq", "exp", None),
    )
    return jax.shard_map(shards, mesh=mesh, in_specs=in_specs, out_specs=(token, token, token), check_vma=False)
```

```python
import functools

import jax
import jax.numpy as jnp
import numpy as np
from jax import lax
from jax.experimental import pallas as pl
from jax.experimental.pallas import tpu as pltpu
from jax.sharding import PartitionSpec as P

BF = jnp.bfloat16
F32 = jnp.float32
MESH = pl.DeviceIdType.MESH

D = 5120
LAT = 512
LATW = 576
FB = 192
ROWS = 256
DROWS = 4
TOP = 6
NS = 8
NE = 16
NG = 16
SLOTS = 256
CZ = 3072
CP = D - CZ
HP = CP // 2
MW = (128, 128, 256, 256)
DC = len(MW)
AT = tuple(4 * sum(MW[:i]) for i in range(DC))
META = 128
PIECE = tuple(pl.ds(META * (i > 0) + sum(MW[:i]), MW[i] + META * (i == 0)) for i in range(DC))
GROUP = tuple(pl.ds(META + sum(MW[:i]), MW[i]) for i in range(DC))
RC = 3
RW = CZ // RC
RQ = RW // 4
PQ = 8
PW = CP // PQ

PLANE = ((2, 2), (0, 1), (0, 3), (2, 1), (2, 3), (1, 0), (3, 0), (1, 2), (3, 2), (1, 1), (3, 3), (1, 3), (3, 1), (0, 2), (2, 0))
ZOFF = (4, 3, 5, 2, 6, 1, 7)
COL = ((0, 4), (1, 4), (0, 3), (0, 5), (1, 3), (1, 5), (0, 2), (0, 6), (1, 2), (1, 6), (0, 1), (0, 7), (1, 1), (1, 7), (1, 0))

NT = (((1,), (1,)), ((), ()))


def iota(shape, dim):
    return lax.broadcasted_iota(jnp.int32, shape, dim)


def wait_bytes(ref, sem):
    pltpu.make_async_copy(ref, ref, sem).wait()


def latents(comp, pos, kv_gain, freq):
    lat = comp[:, :LAT]
    ms = jnp.mean(lat * lat, axis=-1, keepdims=True)
    lat = lat * lax.rsqrt(ms + 1e-06) * kv_gain
    rot = comp[:, LAT:]
    angle = pos * freq
    sine = jnp.sin(angle)
    swapped = jnp.concatenate([rot[:, 32:], rot[:, :32]], axis=-1)
    lane = iota(rot.shape, 1)
    rot = rot * jnp.cos(angle) + jnp.where(lane < 32, -sine, sine) * swapped
    return lat, rot


def kernel(
    dh_hbm, ng_hbm, kg_hbm, freq_hbm, ids_hbm, gates_hbm, owner_hbm, plen_hbm, ctx_hbm, ph_hbm, wk_hbm, wg_hbm, wu_hbm, wd_hbm,
    moe_out, newlat_out, cache_out,
    ph, wk, wgu, wd, xp, comp, msg, gath, sbuf, xbuf, hacc, actb, ybuf, rbuf, fbuf, qbuf, pbuf, abuf, bbuf, cbuf,
    mtp, pmsg, parr, pxb, ypb, sumr, suml, gotr, gotl, pfold, pback, wts,
    dh, ng, kg, freq, ids, gates, owner, plen, ctx,
    lsem, zs, zr, ds_, dr, p1s, p1r, p2s, p2r, rs, rr, fs, fr,
    ps, pr, gs, gr, us, ur, bs, br, isem,
):
    h = lax.axis_index("half")
    s = lax.axis_index("seq")
    e = lax.axis_index("exp")
    y = e // 4
    x = e % 4
    g = h * NS + s
    plane_ids = [((y + dy) % 4) * 4 + (x + dx) % 4 for dy, dx in PLANE]
    z_ids = [(s + d) % NS for d in ZOFF]
    col_ids = [((h + dh_) % 2, (s + d) % NS) for dh_, d in COL]

    barrier = pltpu.get_barrier_semaphore()
    for hp, sp in col_ids:
        pl.semaphore_signal(barrier, inc=1, device_id=(hp, sp, e), device_id_type=MESH)
    for p in plane_ids:
        pl.semaphore_signal(barrier, inc=1, device_id=(h, s, p), device_id_type=MESH)

    small = [
        pltpu.make_async_copy(src, dst, isem.at[i]) for i, (src, dst) in enumerate((
            (dh_hbm, dh), (ng_hbm, ng), (ids_hbm, ids), (gates_hbm, gates), (kg_hbm, kg), (freq_hbm, freq),
            (owner_hbm, owner), (plen_hbm, plen), (ctx_hbm, ctx)))
    ]
    for c in small:
        c.start()
    loads = [
        pltpu.make_async_copy(ph_hbm, ph, lsem.at[0]),
        pltpu.make_async_copy(wk_hbm, wk, lsem.at[1]),
        pltpu.make_async_copy(wg_hbm, wgu.at[pl.ds(0, FB)], lsem.at[2]),
        pltpu.make_async_copy(wu_hbm, wgu.at[pl.ds(FB, FB)], lsem.at[3]),
        pltpu.make_async_copy(wd_hbm, wd, lsem.at[4]),
    ]
    for c in loads:
        c.start()

    for c in small:
        c.wait()

    dec = dh[...].astype(F32)
    ms = jnp.mean(dec * dec, axis=-1, keepdims=True)
    dn = dec * lax.rsqrt(ms + 1e-06) * ng[...]
    for at, w, cols in zip(AT, MW, GROUP):
        msg[:, cols] = jnp.concatenate([dn[:, at + q * w:at + (q + 1) * w] for q in range(4)], axis=0).astype(BF)
    xp[pl.ds(ROWS, 16), :] = jnp.concatenate([dn, jnp.zeros((12, D), F32)], axis=0).astype(BF)
    lane = iota((1, META), 1)
    kind = lane // 32
    xl = (lane % 32) // 2
    cl = lane % 2
    before = jnp.zeros((1, META), jnp.int32)
    rows = []
    for r in range(DROWS):
        named = jnp.zeros((1, META), jnp.int32)
        gv = jnp.zeros((1, META), F32)
        for k in range(TOP):
            hit = xl == ids[r, k]
            named = named + jnp.where(hit, 1, 0)
            gv = gv + jnp.where(hit, gates[r, k], 0.0)
        hi = gv.astype(BF).astype(F32)
        val = jnp.where(kind == 0, 1.0, jnp.where(kind == 1, hi, jnp.where(kind == 2, gv - hi, 0.0)))
        rows.append(jnp.where((named > 0) & (before == cl), val, 0.0))
        before = before + named
    meta4 = jnp.concatenate(rows, axis=0)
    msg[:, pl.ds(0, META)] = jnp.concatenate([meta4] * 4, axis=0).astype(BF)

    mtp[...] = jnp.concatenate([meta4] * PQ, axis=0).astype(BF)
    fi = iota((SLOTS, META), 0)
    fj = iota((SLOTS, META), 1)
    fsame = ((fi // 16) == ((fj % 32) // 2)) & (((fi // 8) % 2) == (fj % 2))
    fold_slot = jnp.where(fsame & (fj // 32 == 0), 1.0, 0.0).astype(BF)
    tf = lax.dot_general(fold_slot, mtp[...], NT, preferred_element_type=F32)
    self_ = jnp.where(iota((SLOTS, 4 * PQ), 0) % PQ == iota((SLOTS, 4 * PQ), 1) // 4, tf, 0.0).astype(BF)
    dcols = jnp.concatenate([dn[:, CZ + q * PW:CZ + (q + 1) * PW] for q in range(PQ)], axis=0).astype(BF)
    pmsg[...] = jnp.dot(self_, dcols, preferred_element_type=F32).astype(BF)

    loads[0].wait()

    def pnorm(i, _):
        at = pl.ds(pl.multiple_of(i * 32, 32), 32)
        v = ph[at, :].astype(F32)
        m = jnp.mean(v * v, axis=-1, keepdims=True)
        xp[at, :] = (v * lax.rsqrt(m + 1e-06) * ng[...]).astype(BF)
        return 0

    lax.fori_loop(0, ROWS // 32, pnorm, 0)

    pl.semaphore_wait(barrier, len(PLANE) + len(COL))

    my_rows = pl.ds(pl.multiple_of(s * 16, 16), 16)
    own = pl.ds(pl.multiple_of(e * 16, 16), 16)
    for i, cols in enumerate(PIECE):
        for p in z_ids:
            pltpu.make_async_remote_copy(
                msg.at[:, cols], gath.at[my_rows, cols], zs.at[i], zr.at[i], device_id=(h, p, e), device_id_type=MESH).start()
    for p in plane_ids:
        pltpu.make_async_remote_copy(
            pmsg.at[pl.ds(pl.multiple_of(p * 16, 16), 16)], parr.at[own], ps, pr,
            device_id=(h, s, p), device_id_type=MESH).start()
    gath[my_rows, :] = msg[...]
    parr[own, :] = pmsg[own, :]

    right = (s + 1) % NS
    left = (s + 7) % NS

    sides = (right, left)
    halves = (pl.ds(0, HP), pl.ds(HP, HP))

    def block(d, t):
        return (s + NS - t) % NS if d == 0 else (s + t) % NS

    def gather_send(d, t, u):
        if t > 0:
            wait_bytes(pxb.at[block(d, t), :, halves[u]], gr.at[d, t - 1, u])
        part = pxb.at[block(d, t), :, halves[u]]
        pltpu.make_async_remote_copy(
            part, part, gs.at[d, t, u], gr.at[d, t, u], device_id=(h, sides[d], e), device_id_type=MESH).start()

    def gather_step(t):
        for d in range(2):
            gather_send(d, t, d)
        if t < 3:
            for d in range(2):
                gather_send(d, t, 1 - d)

    def gather_end():
        for d in range(2):
            wait_bytes(pxb.at[block(d, 4), :, halves[d]], gr.at[d, 3, d])
            wait_bytes(pxb.at[block(d, 3), :, halves[1 - d]], gr.at[d, 2, 1 - d])

    loads[1].wait()
    comp[...] = jnp.zeros_like(comp)

    def compress(i, _):
        at = pl.ds(pl.multiple_of(i * 1024, 1024), 1024)
        comp[...] += lax.dot_general(xp[:, at], wk[:, at], NT, preferred_element_type=F32)
        return 0

    lax.fori_loop(0, D // 1024, compress, 0)
    length = plen[g * NE + e]

    def prompt_latents(i, _):
        at = pl.ds(pl.multiple_of(i * 64, 64), 64)
        rid = iota((64, 1), 0) + i * 64
        lat, rot = latents(comp[at, :], rid.astype(F32), kg[...], freq[...])
        pbuf[at, pl.ds(0, LAT)] = jnp.where(rid < length, lat, 0.0).astype(BF)
        pbuf[at, pl.ds(LAT, 64)] = jnp.where(rid < length, rot, 0.0).astype(BF)
        return 0

    lax.fori_loop(0, ROWS // 64, prompt_latents, 0)

    ui = iota((SLOTS, SLOTS), 0)
    uj = iota((SLOTS, SLOTS), 1)
    unfold = jnp.where(uj == ((ui % 32) // 2) * 16 + (ui % 2) * 8 + ui // 32, 1.0, 0.0).astype(BF)
    wait_bytes(parr.at[pl.ds(0, 240)], pr)
    flat = jnp.dot(unfold, parr[...], preferred_element_type=F32).astype(BF)
    for q in range(PQ):
        pxb[s, :, pl.ds(q * PW, PW)] = flat[q * 32:(q + 1) * 32, :]
    gather_step(0)
    mine = pl.ds(pl.multiple_of(g * 16, 16), 16)
    for hp, sp in col_ids:
        pltpu.make_async_remote_copy(
            pbuf.at[pl.ds(pl.multiple_of((hp * NS + sp) * 16, 16), 16)], abuf.at[mine], p1s, p1r,
            device_id=(hp, sp, e), device_id_type=MESH).start()
    abuf[mine, :] = pbuf[mine, :]


    wait_bytes(gath.at[pl.ds(0, 112), PIECE[0]], zr.at[0])
    mt = gath[:, pl.ds(0, META)]
    ei = iota((SLOTS, META), 0)
    ej = iota((SLOTS, META), 1)
    same = ((ei // 16) == ((ej % 32) // 2)) & ((ei % 2) == (ej % 2))
    et_slot = jnp.where(same & (ej // 32 == 0), 1.0, 0.0).astype(BF)
    et_gate = jnp.where(same & ((ej // 32 == 1) | (ej // 32 == 2)), 1.0, 0.0).astype(BF)
    t2 = lax.dot_general(et_slot, mt, NT, preferred_element_type=F32)
    samez = ((ei // 2) % 8) == (ej // 16)

    def dispatch(c):
        if c > 0:
            wait_bytes(gath.at[pl.ds(0, 112), PIECE[c]], zr.at[c])
        for q in range(4):
            pick = jnp.where(samez & ((ej // 4) % 4 == q), t2, 0.0).astype(BF)
            sbuf[:, pl.ds(AT[c] + q * MW[c], MW[c])] = jnp.dot(
                pick, gath[:, GROUP[c]], preferred_element_type=F32).astype(BF)
        cols = pl.ds(AT[c], 4 * MW[c])
        for p in plane_ids:
            pltpu.make_async_remote_copy(
                sbuf.at[pl.ds(pl.multiple_of(p * 16, 16), 16), cols], xbuf.at[own, cols], ds_.at[c], dr.at[c],
                device_id=(h, s, p), device_id_type=MESH).start()
        xbuf[own, cols] = sbuf[own, cols]

    dispatch(0)
    dispatch(1)
    gather_step(1)
    dispatch(2)
    dispatch(3)
    gather_step(2)

    cg = lax.dot_general(mt, et_gate, NT, preferred_element_type=F32)
    ci = iota((META, SLOTS), 0)
    cj = iota((META, SLOTS), 1)
    cz = (ci // 16) == ((cj // 2) % 8)
    for q in range(4):
        w = jnp.where(cz & ((ci // 4) % 4 == q), cg, 0.0)
        hi = w.astype(BF)
        wts[q] = hi
        wts[q + 4] = (w - hi.astype(F32)).astype(BF)
    rid = iota((16, 1), 0)
    dpos = jnp.where(rid < 2, ctx[0, 0], ctx[0, 1]) + rid % 2
    lat, rot = latents(comp[pl.ds(ROWS, 16), :], dpos.astype(F32), kg[...], freq[...])
    newlat_out[:, pl.ds(0, LAT)] = lat[:DROWS].astype(BF)
    newlat_out[:, pl.ds(LAT, 64)] = rot[:DROWS].astype(BF)

    gather_step(3)

    lane = iota((1, ROWS), 1)
    to = jnp.zeros((1, ROWS), jnp.int32)
    for k in range(NG):
        to = to + jnp.where(lane // 16 == k, owner[e, k], 0)
    pi = iota((ROWS, ROWS), 0)
    pj = iota((ROWS, ROWS), 1)
    perm = jnp.where((pi // 16 == to) & (pi % 16 == pj % 16), 1.0, 0.0).astype(BF)
    loads[2].wait()
    loads[3].wait()
    hacc[...] = jnp.zeros_like(hacc)

    def up(c):
        cols = pl.ds(AT[c], 4 * MW[c])
        wait_bytes(xbuf.at[pl.ds(0, 240), cols], dr.at[c])
        hacc[...] += lax.dot_general(xbuf[:, cols], wgu[:, cols], NT, preferred_element_type=F32)

    for c in range(DC - 1):
        up(c)
    gather_end()
    order = jnp.where(
        ((ui // 16) == ((uj % 32) // 2)) & (((ui // 2) % 8) == uj // 32) & ((ui % 2) == (uj % 2)), 1.0, 0.0).astype(BF)
    back = jnp.where(
        ((uj // 16) == ((ui % 32) // 2)) & (((uj // 2) % 8) == ui // 32) & ((uj % 2) == (ui % 2)), 1.0, 0.0).astype(BF)
    hp_ = lax.dot_general(pxb[...].reshape(SLOTS, CP), wgu[:, pl.ds(CZ, CP)], NT, preferred_element_type=F32)
    hp_hi = hp_.astype(BF)
    hp_lo = (hp_ - hp_hi.astype(F32)).astype(BF)
    hacc[...] += jnp.dot(order, hp_hi, preferred_element_type=F32) + jnp.dot(order, hp_lo, preferred_element_type=F32)
    wait_bytes(abuf.at[pl.ds(0, 240)], p1r)
    bbuf[...] = jnp.dot(perm, abuf[...], preferred_element_type=F32).astype(BF)
    for hp, sp in col_ids:
        pltpu.make_async_remote_copy(
            bbuf.at[pl.ds(pl.multiple_of((hp * NS + sp) * 16, 16), 16)], cbuf.at[mine], p2s, p2r,
            device_id=(hp, sp, e), device_id_type=MESH).start()
    cbuf[mine, :] = bbuf[mine, :]

    up(DC - 1)
    gate = hacc[:, pl.ds(0, FB)]
    actb[...] = (gate * jax.nn.sigmoid(gate) * hacc[:, pl.ds(FB, FB)]).astype(BF)
    loads[4].wait()

    def down(k, _):
        at = pl.ds(pl.multiple_of(k * RW, RW), RW)
        ybuf[k] = jnp.dot(actb[...], wd[:, at], preferred_element_type=F32).astype(BF)
        for p in plane_ids:
            pltpu.make_async_remote_copy(
                ybuf.at[k, pl.ds(pl.multiple_of(p * 16, 16), 16)], rbuf.at[k, own], rs.at[k], rr.at[k],
                device_id=(h, s, p), device_id_type=MESH).start()
        rbuf[k, own, :] = ybuf[k, own, :]
        return 0

    down(0, 0)

    actp = jnp.dot(back, actb[...], preferred_element_type=F32).astype(BF)
    ypb[...] = jnp.dot(actp, wd[:, pl.ds(CZ, CP)], preferred_element_type=F32).astype(BF).reshape(NS, 32, CP)
    got = (gotr, gotl)
    summed = (sumr, suml)

    def sum_send(d, t, u):
        dest = (s + 4 - t) % NS if d == 0 else (s + 4 + t) % NS
        at = halves[u]
        if t == (0 if u == d else 1):
            src = ypb.at[dest, :, at]
        else:
            wait_bytes(got[d].at[t - 1, :, at], ur.at[d, t - 1, u])
            summed[d][t - 1, :, at] = (ypb[dest, :, at].astype(F32) + got[d][t - 1, :, at].astype(F32)).astype(BF)
            src = summed[d].at[t - 1, :, at]
        pltpu.make_async_remote_copy(
            src, got[d].at[t, :, at], us.at[d, t, u], ur.at[d, t, u],
            device_id=(h, sides[d], e), device_id_type=MESH).start()

    for d in range(2):
        sum_send(d, 0, d)
    for d in range(2):
        sum_send(d, 1, 1 - d)
    for k in range(1, RC):
        down(k, 0)

    def sum_step(t):
        for d in range(2):
            sum_send(d, t, d)
        if t < 3:
            for d in range(2):
                sum_send(d, t + 1, 1 - d)


    def combine(k, _):
        wait_bytes(rbuf.at[k, pl.ds(0, 240)], rr.at[k])
        total = jnp.zeros((META, RQ), F32)
        for q in range(4):
            part = rbuf[k, :, pl.ds(q * RQ, RQ)]
            total += jnp.dot(wts[q], part, preferred_element_type=F32)
            total += jnp.dot(wts[q + 4], part, preferred_element_type=F32)
        fbuf[k] = total.astype(BF)
        for p in z_ids:
            pltpu.make_async_remote_copy(
                fbuf.at[k, pl.ds(pl.multiple_of(p * 16, 16), 16)], qbuf.at[k, my_rows], fs.at[k], fr.at[k],
                device_id=(h, p, e), device_id_type=MESH).start()
        qbuf[k, my_rows, :] = fbuf[k, my_rows, :]
        return 0

    sum_step(1)
    sum_step(2)
    for k in range(RC - 2):
        combine(k, 0)
    sum_step(3)
    for k in range(RC - 2, RC):
        combine(k, 0)
    for d in range(2):
        for u in range(2):
            wait_bytes(got[d].at[3, :, halves[u]], ur.at[d, 3, u])
    done = (ypb[s].astype(F32) + gotr[3].astype(F32) + gotl[3].astype(F32)).astype(BF)
    stacked = jnp.concatenate([done[:, q * PW:(q + 1) * PW] for q in range(PQ)], axis=0)
    refold = jnp.where(ui == ((uj % 32) // 2) * 16 + (uj % 2) * 8 + uj // 32, 1.0, 0.0).astype(BF)
    pfold[...] = jnp.dot(refold, stacked, preferred_element_type=F32).astype(BF)
    for p in plane_ids:
        pltpu.make_async_remote_copy(
            pfold.at[pl.ds(pl.multiple_of(p * 16, 16), 16)], pback.at[own], bs, br,
            device_id=(h, s, p), device_id_type=MESH).start()
    pback[own, :] = pfold[own, :]
    wait_bytes(cbuf.at[pl.ds(0, 240)], p2r)
    cache_out[...] = cbuf[...].astype(F32).T.astype(BF)


    fold_gate = jnp.where(fsame & ((fj // 32 == 1) | (fj // 32 == 2)), 1.0, 0.0).astype(BF)
    cp = lax.dot_general(mtp[...], fold_gate, NT, preferred_element_type=F32)
    cp = jnp.where(iota((4 * PQ, SLOTS), 1) % PQ == iota((4 * PQ, SLOTS), 0) // 4, cp, 0.0)
    cp_hi = cp.astype(BF)
    cp_lo = (cp - cp_hi.astype(F32)).astype(BF)
    wait_bytes(pback.at[pl.ds(0, 240)], br)
    ptot = jnp.dot(cp_hi, pback[...], preferred_element_type=F32) + jnp.dot(cp_lo, pback[...], preferred_element_type=F32)
    for q in range(PQ):
        moe_out[:, pl.ds(CZ + q * PW, PW)] = ptot[q * 4:q * 4 + 4, :].astype(BF)

    for k in range(RC):
        wait_bytes(qbuf.at[k, pl.ds(0, 112)], fr.at[k])
        tot = jnp.zeros((16, RQ), F32)
        for z in range(NS):
            tot += qbuf[k, pl.ds(z * 16, 16), :].astype(F32)
        for q in range(4):
            moe_out[:, pl.ds(k * RW + q * RQ, RQ)] = tot[q * 4:q * 4 + 4, :].astype(BF)

    for k in range(RC):
        wait_bytes(fbuf.at[k, pl.ds(0, 112)], fs.at[k])
        wait_bytes(ybuf.at[k, pl.ds(0, 240)], rs.at[k])
    for c in range(DC):
        wait_bytes(sbuf.at[pl.ds(0, 240), pl.ds(AT[c], 4 * MW[c])], ds_.at[c])
    for i, cols in enumerate(PIECE):
        wait_bytes(gath.at[pl.ds(0, 112), cols], zs.at[i])
    wait_bytes(parr.at[pl.ds(0, 240)], ps)
    wait_bytes(pback.at[pl.ds(0, 240)], bs)
    for d in range(2):
        for u in range(2):
            for t in range(4):
                if u == d or t < 3:
                    wait_bytes(pxb.at[0, :, halves[u]], gs.at[d, t, u])
                if u == d or t > 0:
                    wait_bytes(ypb.at[0, :, halves[u]], us.at[d, t, u])
    wait_bytes(pbuf.at[pl.ds(0, 240)], p1s)
    wait_bytes(bbuf.at[pl.ds(0, 240)], p2s)


def finish(a, b, c, oa, ob, oc):
    oa[...] = a[...]
    ob[...] = b[...]
    oc[...] = c[...]


def shards(
    prompt_hidden, decode_hidden, norm_gain, w_dkv, kv_gain, w_gate, w_up, w_down, expert_ids, gate_values,
    owner, prompt_lengths, context_lengths,
):
    freq = 10000.0 ** (-(np.arange(32, dtype=np.float64) * 2.0 / 64))
    freq = jnp.asarray(np.concatenate([freq, freq])[None, :], F32)
    vm = pl.BlockSpec(memory_space=pltpu.VMEM)
    hbm = pl.BlockSpec(memory_space=pl.ANY)
    dma = pltpu.SemaphoreType.DMA
    moe, newlat, cache = pl.pallas_call(
        kernel,
        out_shape=(
            jax.ShapeDtypeStruct((DROWS, D), BF),
            jax.ShapeDtypeStruct((DROWS, LATW), BF),
            jax.ShapeDtypeStruct((LATW, ROWS), BF),
        ),
        in_specs=[hbm] * 14,
        out_specs=(vm, vm, vm),
        scratch_shapes=[
            pltpu.VMEM((ROWS, D), BF),
            pltpu.VMEM((LATW, D), BF),
            pltpu.VMEM((2 * FB, D), BF),
            pltpu.VMEM((FB, D), BF),
            pltpu.VMEM((ROWS + 16, D), BF),
            pltpu.VMEM((ROWS + 16, LATW), F32),
            pltpu.VMEM((16, sum(MW) + META), BF),
            pltpu.VMEM((NS * 16, sum(MW) + META), BF),
            pltpu.VMEM((SLOTS, CZ), BF),
            pltpu.VMEM((SLOTS, CZ), BF),
            pltpu.VMEM((SLOTS, 2 * FB), F32),
            pltpu.VMEM((SLOTS, FB), BF),
            pltpu.VMEM((RC, SLOTS, RW), BF),
            pltpu.VMEM((RC, SLOTS, RW), BF),
            pltpu.VMEM((RC, NS * 16, RQ), BF),
            pltpu.VMEM((RC, NS * 16, RQ), BF),
            pltpu.VMEM((ROWS, LATW), BF),
            pltpu.VMEM((ROWS, LATW), BF),
            pltpu.VMEM((ROWS, LATW), BF),
            pltpu.VMEM((ROWS, LATW), BF),
            pltpu.VMEM((4 * PQ, META), BF),
            pltpu.VMEM((SLOTS, PW), BF),
            pltpu.VMEM((SLOTS, PW), BF),
            pltpu.VMEM((NS, 32, CP), BF),
            pltpu.VMEM((NS, 32, CP), BF),
            pltpu.VMEM((3, 32, CP), BF),
            pltpu.VMEM((3, 32, CP), BF),
            pltpu.VMEM((4, 32, CP), BF),
            pltpu.VMEM((4, 32, CP), BF),
            pltpu.VMEM((SLOTS, PW), BF),
            pltpu.VMEM((SLOTS, PW), BF),
            pltpu.VMEM((8, META, SLOTS), BF),
            pltpu.VMEM((DROWS, D), BF),
            pltpu.VMEM((1, D), F32),
            pltpu.VMEM((1, LAT), F32),
            pltpu.VMEM((1, 64), F32),
            pltpu.SMEM((DROWS, TOP), jnp.int32),
            pltpu.SMEM((DROWS, TOP), F32),
            pltpu.SMEM((NG, NE), jnp.int32),
            pltpu.SMEM((NG * NE,), jnp.int32),
            pltpu.SMEM((1, 2), jnp.int32),
            dma((5,)), dma((DC,)), dma((DC,)), dma((DC,)), dma((DC,)), dma, dma, dma, dma, dma((RC,)), dma((RC,)), dma((RC,)), dma((RC,)),
            dma, dma, dma((2, 4, 2)), dma((2, 4, 2)), dma((2, 4, 2)), dma((2, 4, 2)), dma, dma, dma((9,)),
        ],
        compiler_params=pltpu.CompilerParams(collective_id=0, has_side_effects=True, vmem_limit_bytes=56 * 2**20),
        cost_estimate=pl.CostEstimate(flops=4 * 10**9, bytes_accessed=16 * 10**6, transcendentals=10**5),
        name="layer_slice",
    )(
        decode_hidden.reshape(DROWS, D), norm_gain.reshape(1, D), kv_gain.reshape(1, LAT), freq,
        expert_ids.reshape(DROWS, TOP), gate_values.reshape(DROWS, TOP), owner, prompt_lengths,
        context_lengths.reshape(1, 2),
        prompt_hidden.reshape(ROWS, D), w_dkv.T, w_gate[0].T, w_up[0].T, w_down[0],
    )
    moe, newlat, cache = pl.pallas_call(
        finish,
        out_shape=tuple(jax.ShapeDtypeStruct(v.shape, v.dtype) for v in (moe, newlat, cache)),
        in_specs=[vm] * 3,
        out_specs=(vm,) * 3,
        name="results",
    )(moe, newlat, cache)
    return (
        moe.reshape(1, 1, 1, DROWS, D),
        newlat.reshape(1, 1, 1, DROWS, LATW),
        cache.T.reshape(1, 1, 1, ROWS, LATW),
    )


def solution(mesh):
    token = P("half", "seq", "exp", None, None)
    in_specs = (
        token, token, P(), P(), P(), P("exp", None, "seq"), P("exp", None, "seq"), P("exp", "seq", None),
        token, token, P(), P(), P("half", "seq", "exp", None),
    )
    return jax.shard_map(shards, mesh=mesh, in_specs=in_specs, out_specs=(token, token, token), check_vma=False)
```

```python
import functools

import jax
import jax.numpy as jnp
import numpy as np
from jax import lax
from jax.experimental import pallas as pl
from jax.experimental.pallas import tpu as pltpu
from jax.sharding import PartitionSpec as P

BF = jnp.bfloat16
F32 = jnp.float32
MESH = pl.DeviceIdType.MESH

D = 5120
LAT = 512
LATW = 576
FB = 192
ROWS = 256
DROWS = 4
TOP = 6
NS = 8
NE = 16
NG = 16
SLOTS = 256
CZ = 3072
CP = D - CZ
HP = CP // 2
MW = (128, 128, 256, 256)
DC = len(MW)
AT = tuple(4 * sum(MW[:i]) for i in range(DC))
META = 128
PIECE = tuple(pl.ds(META * (i > 0) + sum(MW[:i]), MW[i] + META * (i == 0)) for i in range(DC))
GROUP = tuple(pl.ds(META + sum(MW[:i]), MW[i]) for i in range(DC))
RC = 3
RW = CZ // RC
RQ = RW // 4
PQ = 8
PW = CP // PQ

PLANE = ((2, 2), (0, 1), (0, 3), (2, 1), (2, 3), (1, 0), (3, 0), (1, 2), (3, 2), (1, 1), (3, 3), (1, 3), (3, 1), (0, 2), (2, 0))
ZOFF = (4, 3, 5, 2, 6, 1, 7)
COL = ((0, 4), (1, 4), (0, 3), (0, 5), (1, 3), (1, 5), (0, 2), (0, 6), (1, 2), (1, 6), (0, 1), (0, 7), (1, 1), (1, 7), (1, 0))

NT = (((1,), (1,)), ((), ()))


def iota(shape, dim):
    return lax.broadcasted_iota(jnp.int32, shape, dim)


def wait_bytes(ref, sem):
    pltpu.make_async_copy(ref, ref, sem).wait()


def latents(comp, pos, kv_gain, freq):
    lat = comp[:, :LAT]
    ms = jnp.mean(lat * lat, axis=-1, keepdims=True)
    lat = lat * lax.rsqrt(ms + 1e-06) * kv_gain
    rot = comp[:, LAT:]
    angle = pos * freq
    sine = jnp.sin(angle)
    swapped = jnp.concatenate([rot[:, 32:], rot[:, :32]], axis=-1)
    lane = iota(rot.shape, 1)
    rot = rot * jnp.cos(angle) + jnp.where(lane < 32, -sine, sine) * swapped
    return lat, rot


def kernel(
    dh_hbm, ng_hbm, kg_hbm, freq_hbm, ids_hbm, gates_hbm, owner_hbm, plen_hbm, ctx_hbm, ph_hbm, wk_hbm, wg_hbm, wu_hbm, wd_hbm,
    moe_out, newlat_out, cache_out,
    ph, wk, wgu, wd, xp, comp, msg, gath, sbuf, xbuf, hacc, actb, ybuf, rbuf, fbuf, qbuf, pbuf, abuf, bbuf, cbuf,
    mtp, pmsg, parr, pxb, ypb, sumr, suml, gotr, gotl, pfold, pback, wts,
    dh, ng, kg, freq, ids, gates, owner, plen, ctx,
    lsem, zs, zr, ds_, dr, p1s, p1r, p2s, p2r, rs, rr, fs, fr,
    ps, pr, gs, gr, us, ur, bs, br, isem,
):
    h = lax.axis_index("half")
    s = lax.axis_index("seq")
    e = lax.axis_index("exp")
    y = e // 4
    x = e % 4
    g = h * NS + s
    plane_ids = [((y + dy) % 4) * 4 + (x + dx) % 4 for dy, dx in PLANE]
    z_ids = [(s + d) % NS for d in ZOFF]
    col_ids = [((h + dh_) % 2, (s + d) % NS) for dh_, d in COL]

    barrier = pltpu.get_barrier_semaphore()
    for hp, sp in col_ids:
        pl.semaphore_signal(barrier, inc=1, device_id=(hp, sp, e), device_id_type=MESH)
    for p in plane_ids:
        pl.semaphore_signal(barrier, inc=1, device_id=(h, s, p), device_id_type=MESH)

    small = [
        pltpu.make_async_copy(src, dst, isem.at[i]) for i, (src, dst) in enumerate((
            (dh_hbm, dh), (ng_hbm, ng), (ids_hbm, ids), (gates_hbm, gates), (kg_hbm, kg), (freq_hbm, freq),
            (owner_hbm, owner), (plen_hbm, plen), (ctx_hbm, ctx)))
    ]
    for c in small:
        c.start()
    loads = [
        pltpu.make_async_copy(ph_hbm, ph, lsem.at[0]),
        pltpu.make_async_copy(wk_hbm, wk, lsem.at[1]),
        pltpu.make_async_copy(wg_hbm, wgu.at[pl.ds(0, FB)], lsem.at[2]),
        pltpu.make_async_copy(wu_hbm, wgu.at[pl.ds(FB, FB)], lsem.at[3]),
        pltpu.make_async_copy(wd_hbm, wd, lsem.at[4]),
    ]
    for c in loads:
        c.start()

    for c in small:
        c.wait()

    dec = dh[...].astype(F32)
    ms = jnp.mean(dec * dec, axis=-1, keepdims=True)
    dn = dec * lax.rsqrt(ms + 1e-06) * ng[...]
    for at, w, cols in zip(AT, MW, GROUP):
        msg[:, cols] = jnp.concatenate([dn[:, at + q * w:at + (q + 1) * w] for q in range(4)], axis=0).astype(BF)
    xp[pl.ds(ROWS, 16), :] = jnp.concatenate([dn, jnp.zeros((12, D), F32)], axis=0).astype(BF)
    lane = iota((1, META), 1)
    kind = lane // 32
    xl = (lane % 32) // 2
    cl = lane % 2
    before = jnp.zeros((1, META), jnp.int32)
    rows = []
    for r in range(DROWS):
        named = jnp.zeros((1, META), jnp.int32)
        gv = jnp.zeros((1, META), F32)
        for k in range(TOP):
            hit = xl == ids[r, k]
            named = named + jnp.where(hit, 1, 0)
            gv = gv + jnp.where(hit, gates[r, k], 0.0)
        hi = gv.astype(BF).astype(F32)
        val = jnp.where(kind == 0, 1.0, jnp.where(kind == 1, hi, jnp.where(kind == 2, gv - hi, 0.0)))
        rows.append(jnp.where((named > 0) & (before == cl), val, 0.0))
        before = before + named
    meta4 = jnp.concatenate(rows, axis=0)
    msg[:, pl.ds(0, META)] = jnp.concatenate([meta4] * 4, axis=0).astype(BF)

    mtp[...] = jnp.concatenate([meta4] * PQ, axis=0).astype(BF)
    fi = iota((SLOTS, META), 0)
    fj = iota((SLOTS, META), 1)
    fsame = ((fi // 16) == ((fj % 32) // 2)) & (((fi // 8) % 2) == (fj % 2))
    fold_slot = jnp.where(fsame & (fj // 32 == 0), 1.0, 0.0).astype(BF)
    tf = lax.dot_general(fold_slot, mtp[...], NT, preferred_element_type=F32)
    self_ = jnp.where(iota((SLOTS, 4 * PQ), 0) % PQ == iota((SLOTS, 4 * PQ), 1) // 4, tf, 0.0).astype(BF)
    dcols = jnp.concatenate([dn[:, CZ + q * PW:CZ + (q + 1) * PW] for q in range(PQ)], axis=0).astype(BF)
    pmsg[...] = jnp.dot(self_, dcols, preferred_element_type=F32).astype(BF)

    loads[0].wait()

    def pnorm(i, _):
        at = pl.ds(pl.multiple_of(i * 32, 32), 32)
        v = ph[at, :].astype(F32)
        m = jnp.mean(v * v, axis=-1, keepdims=True)
        xp[at, :] = (v * lax.rsqrt(m + 1e-06) * ng[...]).astype(BF)
        return 0

    lax.fori_loop(0, ROWS // 32, pnorm, 0)

    pl.semaphore_wait(barrier, len(PLANE) + len(COL))

    my_rows = pl.ds(pl.multiple_of(s * 16, 16), 16)
    own = pl.ds(pl.multiple_of(e * 16, 16), 16)
    def send_piece(i):
        for p in z_ids:
            pltpu.make_async_remote_copy(
                msg.at[:, PIECE[i]], gath.at[my_rows, PIECE[i]], zs.at[i], zr.at[i],
                device_id=(h, p, e), device_id_type=MESH).start()

    send_piece(0)
    for p in plane_ids:
        pltpu.make_async_remote_copy(
            pmsg.at[pl.ds(pl.multiple_of(p * 16, 16), 16)], parr.at[own], ps, pr,
            device_id=(h, s, p), device_id_type=MESH).start()
    for i in range(1, DC):
        send_piece(i)
    gath[my_rows, :] = msg[...]
    parr[own, :] = pmsg[own, :]

    right = (s + 1) % NS
    left = (s + 7) % NS

    sides = (right, left)
    halves = (pl.ds(0, HP), pl.ds(HP, HP))

    def block(d, t):
        return (s + NS - t) % NS if d == 0 else (s + t) % NS

    def gather_send(d, t, u):
        if t > 0:
            wait_bytes(pxb.at[block(d, t), :, halves[u]], gr.at[d, t - 1, u])
        part = pxb.at[block(d, t), :, halves[u]]
        pltpu.make_async_remote_copy(
            part, part, gs.at[d, t, u], gr.at[d, t, u], device_id=(h, sides[d], e), device_id_type=MESH).start()

    def gather_step(t):
        for d in range(2):
            gather_send(d, t, d)
        if t < 3:
            for d in range(2):
                gather_send(d, t, 1 - d)

    def gather_end():
        for d in range(2):
            wait_bytes(pxb.at[block(d, 4), :, halves[d]], gr.at[d, 3, d])
            wait_bytes(pxb.at[block(d, 3), :, halves[1 - d]], gr.at[d, 2, 1 - d])

    loads[1].wait()
    comp[...] = jnp.zeros_like(comp)

    def compress(i, _):
        at = pl.ds(pl.multiple_of(i * 1024, 1024), 1024)
        comp[...] += lax.dot_general(xp[:, at], wk[:, at], NT, preferred_element_type=F32)
        return 0

    lax.fori_loop(0, D // 1024, compress, 0)
    length = plen[g * NE + e]

    def prompt_latents(i, _):
        at = pl.ds(pl.multiple_of(i * 64, 64), 64)
        rid = iota((64, 1), 0) + i * 64
        lat, rot = latents(comp[at, :], rid.astype(F32), kg[...], freq[...])
        pbuf[at, pl.ds(0, LAT)] = jnp.where(rid < length, lat, 0.0).astype(BF)
        pbuf[at, pl.ds(LAT, 64)] = jnp.where(rid < length, rot, 0.0).astype(BF)
        return 0

    lax.fori_loop(0, ROWS // 64, prompt_latents, 0)

    ui = iota((SLOTS, SLOTS), 0)
    uj = iota((SLOTS, SLOTS), 1)
    unfold = jnp.where(uj == ((ui % 32) // 2) * 16 + (ui % 2) * 8 + ui // 32, 1.0, 0.0).astype(BF)
    wait_bytes(parr.at[pl.ds(0, 240)], pr)
    flat = jnp.dot(unfold, parr[...], preferred_element_type=F32).astype(BF)
    for q in range(PQ):
        pxb[s, :, pl.ds(q * PW, PW)] = flat[q * 32:(q + 1) * 32, :]
    gather_step(0)
    mine = pl.ds(pl.multiple_of(g * 16, 16), 16)
    for hp, sp in col_ids:
        pltpu.make_async_remote_copy(
            pbuf.at[pl.ds(pl.multiple_of((hp * NS + sp) * 16, 16), 16)], abuf.at[mine], p1s, p1r,
            device_id=(hp, sp, e), device_id_type=MESH).start()
    abuf[mine, :] = pbuf[mine, :]


    wait_bytes(gath.at[pl.ds(0, 112), PIECE[0]], zr.at[0])
    mt = gath[:, pl.ds(0, META)]
    ei = iota((SLOTS, META), 0)
    ej = iota((SLOTS, META), 1)
    same = ((ei // 16) == ((ej % 32) // 2)) & ((ei % 2) == (ej % 2))
    et_slot = jnp.where(same & (ej // 32 == 0), 1.0, 0.0).astype(BF)
    et_gate = jnp.where(same & ((ej // 32 == 1) | (ej // 32 == 2)), 1.0, 0.0).astype(BF)
    t2 = lax.dot_general(et_slot, mt, NT, preferred_element_type=F32)
    samez = ((ei // 2) % 8) == (ej // 16)

    def dispatch(c):
        if c > 0:
            wait_bytes(gath.at[pl.ds(0, 112), PIECE[c]], zr.at[c])
        for q in range(4):
            pick = jnp.where(samez & ((ej // 4) % 4 == q), t2, 0.0).astype(BF)
            sbuf[:, pl.ds(AT[c] + q * MW[c], MW[c])] = jnp.dot(
                pick, gath[:, GROUP[c]], preferred_element_type=F32).astype(BF)
        cols = pl.ds(AT[c], 4 * MW[c])
        for p in plane_ids:
            pltpu.make_async_remote_copy(
                sbuf.at[pl.ds(pl.multiple_of(p * 16, 16), 16), cols], xbuf.at[own, cols], ds_.at[c], dr.at[c],
                device_id=(h, s, p), device_id_type=MESH).start()
        xbuf[own, cols] = sbuf[own, cols]

    dispatch(0)
    dispatch(1)
    gather_step(1)
    dispatch(2)
    dispatch(3)
    gather_step(2)

    cg = lax.dot_general(mt, et_gate, NT, preferred_element_type=F32)
    ci = iota((META, SLOTS), 0)
    cj = iota((META, SLOTS), 1)
    cz = (ci // 16) == ((cj // 2) % 8)
    for q in range(4):
        w = jnp.where(cz & ((ci // 4) % 4 == q), cg, 0.0)
        hi = w.astype(BF)
        wts[q] = hi
        wts[q + 4] = (w - hi.astype(F32)).astype(BF)
    rid = iota((16, 1), 0)
    dpos = jnp.where(rid < 2, ctx[0, 0], ctx[0, 1]) + rid % 2
    lat, rot = latents(comp[pl.ds(ROWS, 16), :], dpos.astype(F32), kg[...], freq[...])
    newlat_out[:, pl.ds(0, LAT)] = lat[:DROWS].astype(BF)
    newlat_out[:, pl.ds(LAT, 64)] = rot[:DROWS].astype(BF)

    gather_step(3)

    lane = iota((1, ROWS), 1)
    to = jnp.zeros((1, ROWS), jnp.int32)
    for k in range(NG):
        to = to + jnp.where(lane // 16 == k, owner[e, k], 0)
    pi = iota((ROWS, ROWS), 0)
    pj = iota((ROWS, ROWS), 1)
    perm = jnp.where((pi // 16 == to) & (pi % 16 == pj % 16), 1.0, 0.0).astype(BF)
    wait_bytes(abuf.at[pl.ds(0, 240)], p1r)
    bbuf[...] = jnp.dot(perm, abuf[...], preferred_element_type=F32).astype(BF)
    for hp, sp in col_ids:
        pltpu.make_async_remote_copy(
            bbuf.at[pl.ds(pl.multiple_of((hp * NS + sp) * 16, 16), 16)], cbuf.at[mine], p2s, p2r,
            device_id=(hp, sp, e), device_id_type=MESH).start()
    cbuf[mine, :] = bbuf[mine, :]

    loads[2].wait()
    loads[3].wait()
    hacc[...] = jnp.zeros_like(hacc)

    def up(c):
        cols = pl.ds(AT[c], 4 * MW[c])
        wait_bytes(xbuf.at[pl.ds(0, 240), cols], dr.at[c])
        hacc[...] += lax.dot_general(xbuf[:, cols], wgu[:, cols], NT, preferred_element_type=F32)

    for c in range(DC - 1):
        up(c)
    gather_end()
    order = jnp.where(
        ((ui // 16) == ((uj % 32) // 2)) & (((ui // 2) % 8) == uj // 32) & ((ui % 2) == (uj % 2)), 1.0, 0.0).astype(BF)
    back = jnp.where(
        ((uj // 16) == ((ui % 32) // 2)) & (((uj // 2) % 8) == ui // 32) & ((uj % 2) == (ui % 2)), 1.0, 0.0).astype(BF)
    hp_ = lax.dot_general(pxb[...].reshape(SLOTS, CP), wgu[:, pl.ds(CZ, CP)], NT, preferred_element_type=F32)
    hp_hi = hp_.astype(BF)
    hp_lo = (hp_ - hp_hi.astype(F32)).astype(BF)
    hacc[...] += jnp.dot(order, hp_hi, preferred_element_type=F32) + jnp.dot(order, hp_lo, preferred_element_type=F32)
    up(DC - 1)
    gate = hacc[:, pl.ds(0, FB)]
    actb[...] = (gate * jax.nn.sigmoid(gate) * hacc[:, pl.ds(FB, FB)]).astype(BF)
    loads[4].wait()

    def down(k, _):
        at = pl.ds(pl.multiple_of(k * RW, RW), RW)
        ybuf[k] = jnp.dot(actb[...], wd[:, at], preferred_element_type=F32).astype(BF)
        for p in plane_ids:
            pltpu.make_async_remote_copy(
                ybuf.at[k, pl.ds(pl.multiple_of(p * 16, 16), 16)], rbuf.at[k, own], rs.at[k], rr.at[k],
                device_id=(h, s, p), device_id_type=MESH).start()
        rbuf[k, own, :] = ybuf[k, own, :]
        return 0

    down(0, 0)

    actp = jnp.dot(back, actb[...], preferred_element_type=F32).astype(BF)
    ypb[...] = jnp.dot(actp, wd[:, pl.ds(CZ, CP)], preferred_element_type=F32).astype(BF).reshape(NS, 32, CP)
    got = (gotr, gotl)
    summed = (sumr, suml)

    def sum_send(d, t, u):
        dest = (s + 4 - t) % NS if d == 0 else (s + 4 + t) % NS
        at = halves[u]
        if t == (0 if u == d else 1):
            src = ypb.at[dest, :, at]
        else:
            wait_bytes(got[d].at[t - 1, :, at], ur.at[d, t - 1, u])
            summed[d][t - 1, :, at] = (ypb[dest, :, at].astype(F32) + got[d][t - 1, :, at].astype(F32)).astype(BF)
            src = summed[d].at[t - 1, :, at]
        pltpu.make_async_remote_copy(
            src, got[d].at[t, :, at], us.at[d, t, u], ur.at[d, t, u],
            device_id=(h, sides[d], e), device_id_type=MESH).start()

    for d in range(2):
        sum_send(d, 0, d)
    for d in range(2):
        sum_send(d, 1, 1 - d)
    for k in range(1, RC):
        down(k, 0)

    def sum_step(t):
        for d in range(2):
            sum_send(d, t, d)
        if t < 3:
            for d in range(2):
                sum_send(d, t + 1, 1 - d)


    def combine(k, _):
        wait_bytes(rbuf.at[k, pl.ds(0, 240)], rr.at[k])
        total = jnp.zeros((META, RQ), F32)
        for q in range(4):
            part = rbuf[k, :, pl.ds(q * RQ, RQ)]
            total += jnp.dot(wts[q], part, preferred_element_type=F32)
            total += jnp.dot(wts[q + 4], part, preferred_element_type=F32)
        fbuf[k] = total.astype(BF)
        for p in z_ids:
            pltpu.make_async_remote_copy(
                fbuf.at[k, pl.ds(pl.multiple_of(p * 16, 16), 16)], qbuf.at[k, my_rows], fs.at[k], fr.at[k],
                device_id=(h, p, e), device_id_type=MESH).start()
        qbuf[k, my_rows, :] = fbuf[k, my_rows, :]
        return 0

    sum_step(1)
    sum_step(2)
    sum_step(3)
    combine(0, 0)
    combine(1, 0)
    combine(2, 0)
    for d in range(2):
        for u in range(2):
            wait_bytes(got[d].at[3, :, halves[u]], ur.at[d, 3, u])
    done = (ypb[s].astype(F32) + gotr[3].astype(F32) + gotl[3].astype(F32)).astype(BF)
    stacked = jnp.concatenate([done[:, q * PW:(q + 1) * PW] for q in range(PQ)], axis=0)
    refold = jnp.where(ui == ((uj % 32) // 2) * 16 + (uj % 2) * 8 + uj // 32, 1.0, 0.0).astype(BF)
    pfold[...] = jnp.dot(refold, stacked, preferred_element_type=F32).astype(BF)
    for p in plane_ids:
        pltpu.make_async_remote_copy(
            pfold.at[pl.ds(pl.multiple_of(p * 16, 16), 16)], pback.at[own], bs, br,
            device_id=(h, s, p), device_id_type=MESH).start()
    pback[own, :] = pfold[own, :]
    wait_bytes(cbuf.at[pl.ds(0, 240)], p2r)
    cache_out[...] = cbuf[...].astype(F32).T.astype(BF)


    fold_gate = jnp.where(fsame & ((fj // 32 == 1) | (fj // 32 == 2)), 1.0, 0.0).astype(BF)
    cp = lax.dot_general(mtp[...], fold_gate, NT, preferred_element_type=F32)
    cp = jnp.where(iota((4 * PQ, SLOTS), 1) % PQ == iota((4 * PQ, SLOTS), 0) // 4, cp, 0.0)
    cp_hi = cp.astype(BF)
    cp_lo = (cp - cp_hi.astype(F32)).astype(BF)
    wait_bytes(pback.at[pl.ds(0, 240)], br)
    ptot = jnp.dot(cp_hi, pback[...], preferred_element_type=F32) + jnp.dot(cp_lo, pback[...], preferred_element_type=F32)
    for q in range(PQ):
        moe_out[:, pl.ds(CZ + q * PW, PW)] = ptot[q * 4:q * 4 + 4, :].astype(BF)

    for k in range(RC):
        wait_bytes(qbuf.at[k, pl.ds(0, 112)], fr.at[k])
        tot = jnp.zeros((16, RQ), F32)
        for z in range(NS):
            tot += qbuf[k, pl.ds(z * 16, 16), :].astype(F32)
        for q in range(4):
            moe_out[:, pl.ds(k * RW + q * RQ, RQ)] = tot[q * 4:q * 4 + 4, :].astype(BF)

    for k in range(RC):
        wait_bytes(fbuf.at[k, pl.ds(0, 112)], fs.at[k])
        wait_bytes(ybuf.at[k, pl.ds(0, 240)], rs.at[k])
    for c in range(DC):
        wait_bytes(sbuf.at[pl.ds(0, 240), pl.ds(AT[c], 4 * MW[c])], ds_.at[c])
    for i, cols in enumerate(PIECE):
        wait_bytes(gath.at[pl.ds(0, 112), cols], zs.at[i])
    wait_bytes(parr.at[pl.ds(0, 240)], ps)
    wait_bytes(pback.at[pl.ds(0, 240)], bs)
    for d in range(2):
        for u in range(2):
            for t in range(4):
                if u == d or t < 3:
                    wait_bytes(pxb.at[0, :, halves[u]], gs.at[d, t, u])
                if u == d or t > 0:
                    wait_bytes(ypb.at[0, :, halves[u]], us.at[d, t, u])
    wait_bytes(pbuf.at[pl.ds(0, 240)], p1s)
    wait_bytes(bbuf.at[pl.ds(0, 240)], p2s)


def finish(a, b, c, oa, ob, oc):
    oa[...] = a[...]
    ob[...] = b[...]
    oc[...] = c[...]


def shards(
    prompt_hidden, decode_hidden, norm_gain, w_dkv, kv_gain, w_gate, w_up, w_down, expert_ids, gate_values,
    owner, prompt_lengths, context_lengths,
):
    freq = 10000.0 ** (-(np.arange(32, dtype=np.float64) * 2.0 / 64))
    freq = jnp.asarray(np.concatenate([freq, freq])[None, :], F32)
    vm = pl.BlockSpec(memory_space=pltpu.VMEM)
    hbm = pl.BlockSpec(memory_space=pl.ANY)
    dma = pltpu.SemaphoreType.DMA
    moe, newlat, cache = pl.pallas_call(
        kernel,
        out_shape=(
            jax.ShapeDtypeStruct((DROWS, D), BF),
            jax.ShapeDtypeStruct((DROWS, LATW), BF),
            jax.ShapeDtypeStruct((LATW, ROWS), BF),
        ),
        in_specs=[hbm] * 14,
        out_specs=(vm, vm, vm),
        scratch_shapes=[
            pltpu.VMEM((ROWS, D), BF),
            pltpu.VMEM((LATW, D), BF),
            pltpu.VMEM((2 * FB, D), BF),
            pltpu.VMEM((FB, D), BF),
            pltpu.VMEM((ROWS + 16, D), BF),
            pltpu.VMEM((ROWS + 16, LATW), F32),
            pltpu.VMEM((16, sum(MW) + META), BF),
            pltpu.VMEM((NS * 16, sum(MW) + META), BF),
            pltpu.VMEM((SLOTS, CZ), BF),
            pltpu.VMEM((SLOTS, CZ), BF),
            pltpu.VMEM((SLOTS, 2 * FB), F32),
            pltpu.VMEM((SLOTS, FB), BF),
            pltpu.VMEM((RC, SLOTS, RW), BF),
            pltpu.VMEM((RC, SLOTS, RW), BF),
            pltpu.VMEM((RC, NS * 16, RQ), BF),
            pltpu.VMEM((RC, NS * 16, RQ), BF),
            pltpu.VMEM((ROWS, LATW), BF),
            pltpu.VMEM((ROWS, LATW), BF),
            pltpu.VMEM((ROWS, LATW), BF),
            pltpu.VMEM((ROWS, LATW), BF),
            pltpu.VMEM((4 * PQ, META), BF),
            pltpu.VMEM((SLOTS, PW), BF),
            pltpu.VMEM((SLOTS, PW), BF),
            pltpu.VMEM((NS, 32, CP), BF),
            pltpu.VMEM((NS, 32, CP), BF),
            pltpu.VMEM((3, 32, CP), BF),
            pltpu.VMEM((3, 32, CP), BF),
            pltpu.VMEM((4, 32, CP), BF),
            pltpu.VMEM((4, 32, CP), BF),
            pltpu.VMEM((SLOTS, PW), BF),
            pltpu.VMEM((SLOTS, PW), BF),
            pltpu.VMEM((8, META, SLOTS), BF),
            pltpu.VMEM((DROWS, D), BF),
            pltpu.VMEM((1, D), F32),
            pltpu.VMEM((1, LAT), F32),
            pltpu.VMEM((1, 64), F32),
            pltpu.SMEM((DROWS, TOP), jnp.int32),
            pltpu.SMEM((DROWS, TOP), F32),
            pltpu.SMEM((NG, NE), jnp.int32),
            pltpu.SMEM((NG * NE,), jnp.int32),
            pltpu.SMEM((1, 2), jnp.int32),
            dma((5,)), dma((DC,)), dma((DC,)), dma((DC,)), dma((DC,)), dma, dma, dma, dma, dma((RC,)), dma((RC,)), dma((RC,)), dma((RC,)),
            dma, dma, dma((2, 4, 2)), dma((2, 4, 2)), dma((2, 4, 2)), dma((2, 4, 2)), dma, dma, dma((9,)),
        ],
        compiler_params=pltpu.CompilerParams(collective_id=0, has_side_effects=True, vmem_limit_bytes=56 * 2**20),
        cost_estimate=pl.CostEstimate(flops=4 * 10**9, bytes_accessed=16 * 10**6, transcendentals=10**5),
        name="layer_slice",
    )(
        decode_hidden.reshape(DROWS, D), norm_gain.reshape(1, D), kv_gain.reshape(1, LAT), freq,
        expert_ids.reshape(DROWS, TOP), gate_values.reshape(DROWS, TOP), owner, prompt_lengths,
        context_lengths.reshape(1, 2),
        prompt_hidden.reshape(ROWS, D), w_dkv.T, w_gate[0].T, w_up[0].T, w_down[0],
    )
    moe, newlat, cache = pl.pallas_call(
        finish,
        out_shape=tuple(jax.ShapeDtypeStruct(v.shape, v.dtype) for v in (moe, newlat, cache)),
        in_specs=[vm] * 3,
        out_specs=(vm,) * 3,
        name="results",
    )(moe, newlat, cache)
    return (
        moe.reshape(1, 1, 1, DROWS, D),
        newlat.reshape(1, 1, 1, DROWS, LATW),
        cache.T.reshape(1, 1, 1, ROWS, LATW),
    )


def solution(mesh):
    token = P("half", "seq", "exp", None, None)
    in_specs = (
        token, token, P(), P(), P(), P("exp", None, "seq"), P("exp", None, "seq"), P("exp", "seq", None),
        token, token, P(), P(), P("half", "seq", "exp", None),
    )
    return jax.shard_map(shards, mesh=mesh, in_specs=in_specs, out_specs=(token, token, token), check_vma=False)
```

```python
import functools

import jax
import jax.numpy as jnp
import numpy as np
from jax import lax
from jax.experimental import pallas as pl
from jax.experimental.pallas import tpu as pltpu
from jax.sharding import PartitionSpec as P

BF = jnp.bfloat16
F32 = jnp.float32
MESH = pl.DeviceIdType.MESH

D = 5120
LAT = 512
LATW = 576
FB = 192
ROWS = 256
DROWS = 4
TOP = 6
NS = 8
NE = 16
NG = 16
SLOTS = 256
CZ = 3072
CP = D - CZ
HP = CP // 2
MW = (128, 128, 256, 256)
DC = len(MW)
AT = tuple(4 * sum(MW[:i]) for i in range(DC))
META = 128
PIECE = tuple(pl.ds(META * (i > 0) + sum(MW[:i]), MW[i] + META * (i == 0)) for i in range(DC))
GROUP = tuple(pl.ds(META + sum(MW[:i]), MW[i]) for i in range(DC))
RC = 3
RW = CZ // RC
RQ = RW // 4
PQ = 8
PW = CP // PQ

PLANE = ((2, 2), (0, 1), (0, 3), (2, 1), (2, 3), (1, 0), (3, 0), (1, 2), (3, 2), (1, 1), (3, 3), (1, 3), (3, 1), (0, 2), (2, 0))
ZOFF = (4, 3, 5, 2, 6, 1, 7)
COL = ((0, 4), (1, 4), (0, 3), (0, 5), (1, 3), (1, 5), (0, 2), (0, 6), (1, 2), (1, 6), (0, 1), (0, 7), (1, 1), (1, 7), (1, 0))

NT = (((1,), (1,)), ((), ()))


def iota(shape, dim):
    return lax.broadcasted_iota(jnp.int32, shape, dim)


def wait_bytes(ref, sem):
    pltpu.make_async_copy(ref, ref, sem).wait()


def latents(comp, pos, kv_gain, freq):
    lat = comp[:, :LAT]
    ms = jnp.mean(lat * lat, axis=-1, keepdims=True)
    lat = lat * lax.rsqrt(ms + 1e-06) * kv_gain
    rot = comp[:, LAT:]
    angle = pos * freq
    sine = jnp.sin(angle)
    swapped = jnp.concatenate([rot[:, 32:], rot[:, :32]], axis=-1)
    lane = iota(rot.shape, 1)
    rot = rot * jnp.cos(angle) + jnp.where(lane < 32, -sine, sine) * swapped
    return lat, rot


def kernel(
    dh_hbm, ng_hbm, kg_hbm, freq_hbm, ids_hbm, gates_hbm, owner_hbm, plen_hbm, ctx_hbm, ph_hbm, wk_hbm, wg_hbm, wu_hbm, wd_hbm,
    moe_out, newlat_out, cache_out,
    ph, wk, wgu, wd, xp, comp, msg, gath, sbuf, xbuf, hacc, actb, ybuf, rbuf, fbuf, qbuf, pbuf, abuf, bbuf, cbuf,
    mtp, pmsg, parr, pxb, ypb, sumr, suml, gotr, gotl, pfold, pback, wts,
    dh, ng, kg, freq, ids, gates, owner, plen, ctx,
    lsem, zs, zr, ds_, dr, p1s, p1r, p2s, p2r, rs, rr, fs, fr,
    ps, pr, gs, gr, us, ur, bs, br, isem,
):
    h = lax.axis_index("half")
    s = lax.axis_index("seq")
    e = lax.axis_index("exp")
    y = e // 4
    x = e % 4
    g = h * NS + s
    plane_ids = [((y + dy) % 4) * 4 + (x + dx) % 4 for dy, dx in PLANE]
    z_ids = [(s + d) % NS for d in ZOFF]
    col_ids = [((h + dh_) % 2, (s + d) % NS) for dh_, d in COL]

    barrier = pltpu.get_barrier_semaphore()
    for hp, sp in col_ids:
        pl.semaphore_signal(barrier, inc=1, device_id=(hp, sp, e), device_id_type=MESH)
    for p in plane_ids:
        pl.semaphore_signal(barrier, inc=1, device_id=(h, s, p), device_id_type=MESH)

    small = [
        pltpu.make_async_copy(src, dst, isem.at[i]) for i, (src, dst) in enumerate((
            (dh_hbm, dh), (ng_hbm, ng), (ids_hbm, ids), (gates_hbm, gates), (kg_hbm, kg), (freq_hbm, freq),
            (owner_hbm, owner), (plen_hbm, plen), (ctx_hbm, ctx)))
    ]
    for c in small:
        c.start()
    loads = [
        pltpu.make_async_copy(ph_hbm, ph, lsem.at[0]),
        pltpu.make_async_copy(wk_hbm, wk, lsem.at[1]),
        pltpu.make_async_copy(wg_hbm, wgu.at[pl.ds(0, FB)], lsem.at[2]),
        pltpu.make_async_copy(wu_hbm, wgu.at[pl.ds(FB, FB)], lsem.at[3]),
        pltpu.make_async_copy(wd_hbm, wd, lsem.at[4]),
    ]
    for c in loads:
        c.start()

    for c in small:
        c.wait()

    dec = dh[...].astype(F32)
    ms = jnp.mean(dec * dec, axis=-1, keepdims=True)
    dn = dec * lax.rsqrt(ms + 1e-06) * ng[...]
    for at, w, cols in zip(AT, MW, GROUP):
        msg[:, cols] = jnp.concatenate([dn[:, at + q * w:at + (q + 1) * w] for q in range(4)], axis=0).astype(BF)
    xp[pl.ds(ROWS, 16), :] = jnp.concatenate([dn, jnp.zeros((12, D), F32)], axis=0).astype(BF)
    lane = iota((1, META), 1)
    kind = lane // 32
    xl = (lane % 32) // 2
    cl = lane % 2
    before = jnp.zeros((1, META), jnp.int32)
    rows = []
    for r in range(DROWS):
        named = jnp.zeros((1, META), jnp.int32)
        gv = jnp.zeros((1, META), F32)
        for k in range(TOP):
            hit = xl == ids[r, k]
            named = named + jnp.where(hit, 1, 0)
            gv = gv + jnp.where(hit, gates[r, k], 0.0)
        hi = gv.astype(BF).astype(F32)
        val = jnp.where(kind == 0, 1.0, jnp.where(kind == 1, hi, jnp.where(kind == 2, gv - hi, 0.0)))
        rows.append(jnp.where((named > 0) & (before == cl), val, 0.0))
        before = before + named
    meta4 = jnp.concatenate(rows, axis=0)
    msg[:, pl.ds(0, META)] = jnp.concatenate([meta4] * 4, axis=0).astype(BF)

    mtp[...] = jnp.concatenate([meta4] * PQ, axis=0).astype(BF)
    fi = iota((SLOTS, META), 0)
    fj = iota((SLOTS, META), 1)
    fsame = ((fi // 16) == ((fj % 32) // 2)) & (((fi // 8) % 2) == (fj % 2))
    fold_slot = jnp.where(fsame & (fj // 32 == 0), 1.0, 0.0).astype(BF)
    tf = lax.dot_general(fold_slot, mtp[...], NT, preferred_element_type=F32)
    self_ = jnp.where(iota((SLOTS, 4 * PQ), 0) % PQ == iota((SLOTS, 4 * PQ), 1) // 4, tf, 0.0).astype(BF)
    dcols = jnp.concatenate([dn[:, CZ + q * PW:CZ + (q + 1) * PW] for q in range(PQ)], axis=0).astype(BF)
    pmsg[...] = jnp.dot(self_, dcols, preferred_element_type=F32).astype(BF)

    loads[0].wait()

    def pnorm(i, _):
        at = pl.ds(pl.multiple_of(i * 32, 32), 32)
        v = ph[at, :].astype(F32)
        m = jnp.mean(v * v, axis=-1, keepdims=True)
        xp[at, :] = (v * lax.rsqrt(m + 1e-06) * ng[...]).astype(BF)
        return 0

    lax.fori_loop(0, ROWS // 32, pnorm, 0)

    pl.semaphore_wait(barrier, len(PLANE) + len(COL))

    my_rows = pl.ds(pl.multiple_of(s * 16, 16), 16)
    own = pl.ds(pl.multiple_of(e * 16, 16), 16)
    def send_piece(i):
        for p in z_ids:
            pltpu.make_async_remote_copy(
                msg.at[:, PIECE[i]], gath.at[my_rows, PIECE[i]], zs.at[i], zr.at[i],
                device_id=(h, p, e), device_id_type=MESH).start()

    send_piece(0)
    for p in plane_ids:
        pltpu.make_async_remote_copy(
            pmsg.at[pl.ds(pl.multiple_of(p * 16, 16), 16)], parr.at[own], ps, pr,
            device_id=(h, s, p), device_id_type=MESH).start()
    for i in range(1, DC):
        send_piece(i)
    gath[my_rows, :] = msg[...]
    parr[own, :] = pmsg[own, :]

    right = (s + 1) % NS
    left = (s + 7) % NS

    sides = (right, left)
    halves = (pl.ds(0, HP), pl.ds(HP, HP))

    def block(d, t):
        return (s + NS - t) % NS if d == 0 else (s + t) % NS

    def gather_send(d, t, u):
        if t > 0:
            wait_bytes(pxb.at[block(d, t), :, halves[u]], gr.at[d, t - 1, u])
        part = pxb.at[block(d, t), :, halves[u]]
        pltpu.make_async_remote_copy(
            part, part, gs.at[d, t, u], gr.at[d, t, u], device_id=(h, sides[d], e), device_id_type=MESH).start()

    def gather_step(t):
        for d in range(2):
            gather_send(d, t, d)
        if t < 3:
            for d in range(2):
                gather_send(d, t, 1 - d)

    def gather_end():
        for d in range(2):
            wait_bytes(pxb.at[block(d, 4), :, halves[d]], gr.at[d, 3, d])
            wait_bytes(pxb.at[block(d, 3), :, halves[1 - d]], gr.at[d, 2, 1 - d])

    loads[1].wait()
    comp[...] = jnp.zeros_like(comp)

    def compress(i, _):
        at = pl.ds(pl.multiple_of(i * 1024, 1024), 1024)
        comp[...] += lax.dot_general(xp[:, at], wk[:, at], NT, preferred_element_type=F32)
        return 0

    lax.fori_loop(0, D // 1024, compress, 0)
    length = plen[g * NE + e]

    def prompt_latents(i, _):
        at = pl.ds(pl.multiple_of(i * 64, 64), 64)
        rid = iota((64, 1), 0) + i * 64
        lat, rot = latents(comp[at, :], rid.astype(F32), kg[...], freq[...])
        pbuf[at, pl.ds(0, LAT)] = jnp.where(rid < length, lat, 0.0).astype(BF)
        pbuf[at, pl.ds(LAT, 64)] = jnp.where(rid < length, rot, 0.0).astype(BF)
        return 0

    lax.fori_loop(0, ROWS // 64, prompt_latents, 0)

    ui = iota((SLOTS, SLOTS), 0)
    uj = iota((SLOTS, SLOTS), 1)
    unfold = jnp.where(uj == ((ui % 32) // 2) * 16 + (ui % 2) * 8 + ui // 32, 1.0, 0.0).astype(BF)
    wait_bytes(parr.at[pl.ds(0, 240)], pr)
    flat = jnp.dot(unfold, parr[...], preferred_element_type=F32).astype(BF)
    for q in range(PQ):
        pxb[s, :, pl.ds(q * PW, PW)] = flat[q * 32:(q + 1) * 32, :]
    gather_step(0)
    mine = pl.ds(pl.multiple_of(g * 16, 16), 16)
    for hp, sp in col_ids:
        pltpu.make_async_remote_copy(
            pbuf.at[pl.ds(pl.multiple_of((hp * NS + sp) * 16, 16), 16)], abuf.at[mine], p1s, p1r,
            device_id=(hp, sp, e), device_id_type=MESH).start()
    abuf[mine, :] = pbuf[mine, :]


    wait_bytes(gath.at[pl.ds(0, 112), PIECE[0]], zr.at[0])
    mt = gath[:, pl.ds(0, META)]
    ei = iota((SLOTS, META), 0)
    ej = iota((SLOTS, META), 1)
    same = ((ei // 16) == ((ej % 32) // 2)) & ((ei % 2) == (ej % 2))
    et_slot = jnp.where(same & (ej // 32 == 0), 1.0, 0.0).astype(BF)
    et_gate = jnp.where(same & ((ej // 32 == 1) | (ej // 32 == 2)), 1.0, 0.0).astype(BF)
    t2 = lax.dot_general(et_slot, mt, NT, preferred_element_type=F32)
    samez = ((ei // 2) % 8) == (ej // 16)

    def dispatch(c):
        if c > 0:
            wait_bytes(gath.at[pl.ds(0, 112), PIECE[c]], zr.at[c])
        for q in range(4):
            pick = jnp.where(samez & ((ej // 4) % 4 == q), t2, 0.0).astype(BF)
            sbuf[:, pl.ds(AT[c] + q * MW[c], MW[c])] = jnp.dot(
                pick, gath[:, GROUP[c]], preferred_element_type=F32).astype(BF)
        cols = pl.ds(AT[c], 4 * MW[c])
        for p in plane_ids:
            pltpu.make_async_remote_copy(
                sbuf.at[pl.ds(pl.multiple_of(p * 16, 16), 16), cols], xbuf.at[own, cols], ds_.at[c], dr.at[c],
                device_id=(h, s, p), device_id_type=MESH).start()
        xbuf[own, cols] = sbuf[own, cols]

    dispatch(0)
    dispatch(1)
    gather_step(1)
    dispatch(2)
    dispatch(3)
    gather_step(2)

    gather_step(3)

    lane = iota((1, ROWS), 1)
    to = jnp.zeros((1, ROWS), jnp.int32)
    for k in range(NG):
        to = to + jnp.where(lane // 16 == k, owner[e, k], 0)
    pi = iota((ROWS, ROWS), 0)
    pj = iota((ROWS, ROWS), 1)
    perm = jnp.where((pi // 16 == to) & (pi % 16 == pj % 16), 1.0, 0.0).astype(BF)
    wait_bytes(abuf.at[pl.ds(0, 240)], p1r)
    bbuf[...] = jnp.dot(perm, abuf[...], preferred_element_type=F32).astype(BF)
    for hp, sp in col_ids:
        pltpu.make_async_remote_copy(
            bbuf.at[pl.ds(pl.multiple_of((hp * NS + sp) * 16, 16), 16)], cbuf.at[mine], p2s, p2r,
            device_id=(hp, sp, e), device_id_type=MESH).start()
    cbuf[mine, :] = bbuf[mine, :]

    cg = lax.dot_general(mt, et_gate, NT, preferred_element_type=F32)
    ci = iota((META, SLOTS), 0)
    cj = iota((META, SLOTS), 1)
    cz = (ci // 16) == ((cj // 2) % 8)
    for q in range(4):
        w = jnp.where(cz & ((ci // 4) % 4 == q), cg, 0.0)
        hi = w.astype(BF)
        wts[q] = hi
        wts[q + 4] = (w - hi.astype(F32)).astype(BF)
    rid = iota((16, 1), 0)
    dpos = jnp.where(rid < 2, ctx[0, 0], ctx[0, 1]) + rid % 2
    lat, rot = latents(comp[pl.ds(ROWS, 16), :], dpos.astype(F32), kg[...], freq[...])
    newlat_out[:, pl.ds(0, LAT)] = lat[:DROWS].astype(BF)
    newlat_out[:, pl.ds(LAT, 64)] = rot[:DROWS].astype(BF)

    loads[2].wait()
    loads[3].wait()
    hacc[...] = jnp.zeros_like(hacc)

    def up(c):
        cols = pl.ds(AT[c], 4 * MW[c])
        wait_bytes(xbuf.at[pl.ds(0, 240), cols], dr.at[c])
        hacc[...] += lax.dot_general(xbuf[:, cols], wgu[:, cols], NT, preferred_element_type=F32)

    for c in range(DC - 1):
        up(c)
    gather_end()
    order = jnp.where(
        ((ui // 16) == ((uj % 32) // 2)) & (((ui // 2) % 8) == uj // 32) & ((ui % 2) == (uj % 2)), 1.0, 0.0).astype(BF)
    back = jnp.where(
        ((uj // 16) == ((ui % 32) // 2)) & (((uj // 2) % 8) == ui // 32) & ((uj % 2) == (ui % 2)), 1.0, 0.0).astype(BF)
    hp_ = lax.dot_general(pxb[...].reshape(SLOTS, CP), wgu[:, pl.ds(CZ, CP)], NT, preferred_element_type=F32)
    hp_hi = hp_.astype(BF)
    hp_lo = (hp_ - hp_hi.astype(F32)).astype(BF)
    hacc[...] += jnp.dot(order, hp_hi, preferred_element_type=F32) + jnp.dot(order, hp_lo, preferred_element_type=F32)
    up(DC - 1)
    gate = hacc[:, pl.ds(0, FB)]
    actb[...] = (gate * jax.nn.sigmoid(gate) * hacc[:, pl.ds(FB, FB)]).astype(BF)
    loads[4].wait()

    def down(k, _):
        at = pl.ds(pl.multiple_of(k * RW, RW), RW)
        ybuf[k] = jnp.dot(actb[...], wd[:, at], preferred_element_type=F32).astype(BF)
        for p in plane_ids:
            pltpu.make_async_remote_copy(
                ybuf.at[k, pl.ds(pl.multiple_of(p * 16, 16), 16)], rbuf.at[k, own], rs.at[k], rr.at[k],
                device_id=(h, s, p), device_id_type=MESH).start()
        rbuf[k, own, :] = ybuf[k, own, :]
        return 0

    down(0, 0)

    actp = jnp.dot(back, actb[...], preferred_element_type=F32).astype(BF)
    ypb[...] = jnp.dot(actp, wd[:, pl.ds(CZ, CP)], preferred_element_type=F32).astype(BF).reshape(NS, 32, CP)
    got = (gotr, gotl)
    summed = (sumr, suml)

    def sum_send(d, t, u):
        dest = (s + 4 - t) % NS if d == 0 else (s + 4 + t) % NS
        at = halves[u]
        if t == (0 if u == d else 1):
            src = ypb.at[dest, :, at]
        else:
            wait_bytes(got[d].at[t - 1, :, at], ur.at[d, t - 1, u])
            summed[d][t - 1, :, at] = (ypb[dest, :, at].astype(F32) + got[d][t - 1, :, at].astype(F32)).astype(BF)
            src = summed[d].at[t - 1, :, at]
        pltpu.make_async_remote_copy(
            src, got[d].at[t, :, at], us.at[d, t, u], ur.at[d, t, u],
            device_id=(h, sides[d], e), device_id_type=MESH).start()

    for d in range(2):
        sum_send(d, 0, d)
    for d in range(2):
        sum_send(d, 1, 1 - d)
    for k in range(1, RC):
        down(k, 0)

    def sum_step(t):
        for d in range(2):
            sum_send(d, t, d)
        if t < 3:
            for d in range(2):
                sum_send(d, t + 1, 1 - d)


    def combine(k, _):
        wait_bytes(rbuf.at[k, pl.ds(0, 240)], rr.at[k])
        total = jnp.zeros((META, RQ), F32)
        for q in range(4):
            part = rbuf[k, :, pl.ds(q * RQ, RQ)]
            total += jnp.dot(wts[q], part, preferred_element_type=F32)
            total += jnp.dot(wts[q + 4], part, preferred_element_type=F32)
        fbuf[k] = total.astype(BF)
        for p in z_ids:
            pltpu.make_async_remote_copy(
                fbuf.at[k, pl.ds(pl.multiple_of(p * 16, 16), 16)], qbuf.at[k, my_rows], fs.at[k], fr.at[k],
                device_id=(h, p, e), device_id_type=MESH).start()
        qbuf[k, my_rows, :] = fbuf[k, my_rows, :]
        return 0

    sum_step(1)
    sum_step(2)
    sum_step(3)
    combine(0, 0)
    combine(1, 0)
    combine(2, 0)
    for d in range(2):
        for u in range(2):
            wait_bytes(got[d].at[3, :, halves[u]], ur.at[d, 3, u])
    done = (ypb[s].astype(F32) + gotr[3].astype(F32) + gotl[3].astype(F32)).astype(BF)
    stacked = jnp.concatenate([done[:, q * PW:(q + 1) * PW] for q in range(PQ)], axis=0)
    refold = jnp.where(ui == ((uj % 32) // 2) * 16 + (uj % 2) * 8 + uj // 32, 1.0, 0.0).astype(BF)
    pfold[...] = jnp.dot(refold, stacked, preferred_element_type=F32).astype(BF)
    for p in plane_ids:
        pltpu.make_async_remote_copy(
            pfold.at[pl.ds(pl.multiple_of(p * 16, 16), 16)], pback.at[own], bs, br,
            device_id=(h, s, p), device_id_type=MESH).start()
    pback[own, :] = pfold[own, :]
    wait_bytes(cbuf.at[pl.ds(0, 240)], p2r)
    cache_out[...] = cbuf[...].astype(F32).T.astype(BF)


    fold_gate = jnp.where(fsame & ((fj // 32 == 1) | (fj // 32 == 2)), 1.0, 0.0).astype(BF)
    cp = lax.dot_general(mtp[...], fold_gate, NT, preferred_element_type=F32)
    cp = jnp.where(iota((4 * PQ, SLOTS), 1) % PQ == iota((4 * PQ, SLOTS), 0) // 4, cp, 0.0)
    cp_hi = cp.astype(BF)
    cp_lo = (cp - cp_hi.astype(F32)).astype(BF)
    wait_bytes(pback.at[pl.ds(0, 240)], br)
    ptot = jnp.dot(cp_hi, pback[...], preferred_element_type=F32) + jnp.dot(cp_lo, pback[...], preferred_element_type=F32)
    for q in range(PQ):
        moe_out[:, pl.ds(CZ + q * PW, PW)] = ptot[q * 4:q * 4 + 4, :].astype(BF)

    for k in range(RC):
        wait_bytes(qbuf.at[k, pl.ds(0, 112)], fr.at[k])
        tot = jnp.zeros((16, RQ), F32)
        for z in range(NS):
            tot += qbuf[k, pl.ds(z * 16, 16), :].astype(F32)
        for q in range(4):
            moe_out[:, pl.ds(k * RW + q * RQ, RQ)] = tot[q * 4:q * 4 + 4, :].astype(BF)

    for k in range(RC):
        wait_bytes(fbuf.at[k, pl.ds(0, 112)], fs.at[k])
        wait_bytes(ybuf.at[k, pl.ds(0, 240)], rs.at[k])
    for c in range(DC):
        wait_bytes(sbuf.at[pl.ds(0, 240), pl.ds(AT[c], 4 * MW[c])], ds_.at[c])
    for i, cols in enumerate(PIECE):
        wait_bytes(gath.at[pl.ds(0, 112), cols], zs.at[i])
    wait_bytes(parr.at[pl.ds(0, 240)], ps)
    wait_bytes(pback.at[pl.ds(0, 240)], bs)
    for d in range(2):
        for u in range(2):
            for t in range(4):
                if u == d or t < 3:
                    wait_bytes(pxb.at[0, :, halves[u]], gs.at[d, t, u])
                if u == d or t > 0:
                    wait_bytes(ypb.at[0, :, halves[u]], us.at[d, t, u])
    wait_bytes(pbuf.at[pl.ds(0, 240)], p1s)
    wait_bytes(bbuf.at[pl.ds(0, 240)], p2s)


def finish(a, b, c, oa, ob, oc):
    oa[...] = a[...]
    ob[...] = b[...]
    oc[...] = c[...]


def shards(
    prompt_hidden, decode_hidden, norm_gain, w_dkv, kv_gain, w_gate, w_up, w_down, expert_ids, gate_values,
    owner, prompt_lengths, context_lengths,
):
    freq = 10000.0 ** (-(np.arange(32, dtype=np.float64) * 2.0 / 64))
    freq = jnp.asarray(np.concatenate([freq, freq])[None, :], F32)
    vm = pl.BlockSpec(memory_space=pltpu.VMEM)
    hbm = pl.BlockSpec(memory_space=pl.ANY)
    dma = pltpu.SemaphoreType.DMA
    moe, newlat, cache = pl.pallas_call(
        kernel,
        out_shape=(
            jax.ShapeDtypeStruct((DROWS, D), BF),
            jax.ShapeDtypeStruct((DROWS, LATW), BF),
            jax.ShapeDtypeStruct((LATW, ROWS), BF),
        ),
        in_specs=[hbm] * 14,
        out_specs=(vm, vm, vm),
        scratch_shapes=[
            pltpu.VMEM((ROWS, D), BF),
            pltpu.VMEM((LATW, D), BF),
            pltpu.VMEM((2 * FB, D), BF),
            pltpu.VMEM((FB, D), BF),
            pltpu.VMEM((ROWS + 16, D), BF),
            pltpu.VMEM((ROWS + 16, LATW), F32),
            pltpu.VMEM((16, sum(MW) + META), BF),
            pltpu.VMEM((NS * 16, sum(MW) + META), BF),
            pltpu.VMEM((SLOTS, CZ), BF),
            pltpu.VMEM((SLOTS, CZ), BF),
            pltpu.VMEM((SLOTS, 2 * FB), F32),
            pltpu.VMEM((SLOTS, FB), BF),
            pltpu.VMEM((RC, SLOTS, RW), BF),
            pltpu.VMEM((RC, SLOTS, RW), BF),
            pltpu.VMEM((RC, NS * 16, RQ), BF),
            pltpu.VMEM((RC, NS * 16, RQ), BF),
            pltpu.VMEM((ROWS, LATW), BF),
            pltpu.VMEM((ROWS, LATW), BF),
            pltpu.VMEM((ROWS, LATW), BF),
            pltpu.VMEM((ROWS, LATW), BF),
            pltpu.VMEM((4 * PQ, META), BF),
            pltpu.VMEM((SLOTS, PW), BF),
            pltpu.VMEM((SLOTS, PW), BF),
            pltpu.VMEM((NS, 32, CP), BF),
            pltpu.VMEM((NS, 32, CP), BF),
            pltpu.VMEM((3, 32, CP), BF),
            pltpu.VMEM((3, 32, CP), BF),
            pltpu.VMEM((4, 32, CP), BF),
            pltpu.VMEM((4, 32, CP), BF),
            pltpu.VMEM((SLOTS, PW), BF),
            pltpu.VMEM((SLOTS, PW), BF),
            pltpu.VMEM((8, META, SLOTS), BF),
            pltpu.VMEM((DROWS, D), BF),
            pltpu.VMEM((1, D), F32),
            pltpu.VMEM((1, LAT), F32),
            pltpu.VMEM((1, 64), F32),
            pltpu.SMEM((DROWS, TOP), jnp.int32),
            pltpu.SMEM((DROWS, TOP), F32),
            pltpu.SMEM((NG, NE), jnp.int32),
            pltpu.SMEM((NG * NE,), jnp.int32),
            pltpu.SMEM((1, 2), jnp.int32),
            dma((5,)), dma((DC,)), dma((DC,)), dma((DC,)), dma((DC,)), dma, dma, dma, dma, dma((RC,)), dma((RC,)), dma((RC,)), dma((RC,)),
            dma, dma, dma((2, 4, 2)), dma((2, 4, 2)), dma((2, 4, 2)), dma((2, 4, 2)), dma, dma, dma((9,)),
        ],
        compiler_params=pltpu.CompilerParams(collective_id=0, has_side_effects=True, vmem_limit_bytes=56 * 2**20),
        cost_estimate=pl.CostEstimate(flops=4 * 10**9, bytes_accessed=16 * 10**6, transcendentals=10**5),
        name="layer_slice",
    )(
        decode_hidden.reshape(DROWS, D), norm_gain.reshape(1, D), kv_gain.reshape(1, LAT), freq,
        expert_ids.reshape(DROWS, TOP), gate_values.reshape(DROWS, TOP), owner, prompt_lengths,
        context_lengths.reshape(1, 2),
        prompt_hidden.reshape(ROWS, D), w_dkv.T, w_gate[0].T, w_up[0].T, w_down[0],
    )
    moe, newlat, cache = pl.pallas_call(
        finish,
        out_shape=tuple(jax.ShapeDtypeStruct(v.shape, v.dtype) for v in (moe, newlat, cache)),
        in_specs=[vm] * 3,
        out_specs=(vm,) * 3,
        name="results",
    )(moe, newlat, cache)
    return (
        moe.reshape(1, 1, 1, DROWS, D),
        newlat.reshape(1, 1, 1, DROWS, LATW),
        cache.T.reshape(1, 1, 1, ROWS, LATW),
    )


def solution(mesh):
    token = P("half", "seq", "exp", None, None)
    in_specs = (
        token, token, P(), P(), P(), P("exp", None, "seq"), P("exp", None, "seq"), P("exp", "seq", None),
        token, token, P(), P(), P("half", "seq", "exp", None),
    )
    return jax.shard_map(shards, mesh=mesh, in_specs=in_specs, out_specs=(token, token, token), check_vma=False)
```
